32 devices in a mesh: span: 16 (over z, y, x), col: 2 (over core).
Axes of the slice: x: 2, y: 2, z: 4, core: 2. Of those that a mesh axis runs over, the one named last changes fastest.
Arguments:
- adjoint_field: float32 [3, 128, 16, 256], P(None, 'span', None, 'col'), may hold values from -6 to 6
- base_flow: float32 [3, 128, 16, 256], P(None, 'span', None, 'col'), may hold values from -5 to 5
- metric_diag: bfloat16 [3, 128, 16, 256], P(None, 'span', None, 'col'), may hold values from 1 to 2
- metric_cross: bfloat16 [3, 128, 16, 256], P(None, 'span', None, 'col'), may hold values from -0.44921875 to 0.44921875
- jacobian: float32 [128, 16, 256], P('span', None, 'col'), may hold values from 0.5 to 2
Outputs:
- advanced: float32 [3, 128, 16, 256], P(None, 'span', None, 'col')
The draws below stay inside these ranges and needn't reach their ends.
All inputs are finite; a program needn't handle non-finite values.
Results may differ from the reference program's by a relative error of at most 0.0003.
Values sent between devices are 32-bit elements; how exact they have to be, the bound alone decides.
No kernel may reach another device: no remote copies, remote signals or barrier semaphores. Data moves between devices by JAX's collectives and lax.ppermute only.
A program may use at most 64 MiB of HBM per device.

```python
import math
import jax
import jax.numpy as jnp
import numpy as np
from jax import lax

NX = 128
NY = 16
NZ = 256


def steps_of(key, shape, cuts, low, largest):
    factor_of = 1.0
    for dim, parts in cuts:
        draws = jax.random.uniform(jax.random.fold_in(jax.random.fold_in(key, 6), dim), (parts,), jnp.float32, low / len(cuts), largest / len(cuts))
        factor_of = factor_of * jnp.repeat(jnp.exp(draws), shape[dim] // parts).reshape((-1,) + (1,) * (len(shape) - 1 - dim))
    return factor_of


def scatter_about(own_key, dims, width, reach, split=(), kind=jnp.bfloat16):
    values = jax.random.normal(own_key, dims, jnp.float32) * width
    if len(split) > 0:
        values = steps_of(own_key, dims, split, -0.22, 0.18) * values
    return jnp.clip(values, min=-reach, max=reach).astype(kind)


def setup_inputs(seed: int = 0) -> dict:
    splits = jax.random.split(jax.random.key(seed), 6)
    return {
        "adjoint_field": scatter_about(splits[0], (3, NX, NY, NZ), 1.0, 6.0, ((1, 16), (3, 2)), jnp.float32),
        "base_flow": scatter_about(splits[1], (3, NX, NY, NZ), 1.0, 5.0, ((1, 16), (3, 2)), jnp.float32),
        "metric_diag": jnp.clip(1.0 + 1.0 * jax.random.uniform(splits[2], (3, NX, NY, NZ), jnp.float32) ** steps_of(splits[2], (3, NX, NY, NZ), ((1, 16), (3, 2)), -0.2, 0.2), 1.0, 2.0).astype(jnp.bfloat16),
        "metric_cross": jnp.clip(jax.random.uniform(splits[3], (3, NX, NY, NZ), jnp.float32, -0.44921875, 0.44921875) * steps_of(splits[3], (3, NX, NY, NZ), ((1, 16), (3, 2)), -0.4, 0.0), -0.44921875, 0.44921875).astype(jnp.bfloat16),
        "jacobian": jnp.clip(jnp.exp(math.log(2.0) - 1.3862944 * jax.random.uniform(splits[4], (NX, NY, NZ), jnp.float32) ** steps_of(splits[4], (NX, NY, NZ), ((0, 16), (2, 2)), -0.2, 0.2)), 0.5, 2.0),
    }


HIGH = lax.Precision.HIGHEST
VISCOSITY = 0.05
STEP_SIZE = 0.01
GLL_INNER = [-0.8717401485096066, -0.5917001814331423, -0.2092992179024789, 0.2092992179024789, 0.5917001814331423, 0.8717401485096066]
GAUSS_POINTS = [-0.9815606342467192, -0.9041172563704749, -0.7699026741943047, -0.5873179542866175, -0.3678314989981802, -0.1252334085114689, 0.1252334085114689, 0.3678314989981802, 0.5873179542866175, 0.7699026741943047, 0.9041172563704749, 0.9815606342467192]
GAUSS_WEIGHTS = [0.0471753363865118, 0.1069393259953184, 0.1600783285433462, 0.2031674267230659, 0.2334925365383548, 0.2491470458134028, 0.2491470458134028, 0.2334925365383548, 0.2031674267230659, 0.1600783285433462, 0.1069393259953184, 0.0471753363865118]


def legendre_seven(points):
    previous = points * 0.0 + 1.0
    current = points
    for degree in range(1, 7):
        following = ((2.0 * degree + 1.0) * points * current - degree * previous) / (degree + 1.0)
        previous = current
        current = following
    return current


def node_tables():
    gll_nodes = np.array([-1.0] + GLL_INNER + [1.0])
    values = legendre_seven(gll_nodes)
    node_weights = 2.0 / (56.0 * values * values)
    identity = np.eye(8, dtype=bool)
    spacing = gll_nodes[:, None] - gll_nodes[None, :]
    derivative = np.where(identity, 0.0, values[:, None] / (values[None, :] * np.where(identity, 1.0, spacing)))
    corner_terms = np.concatenate([np.array([-14.0]), np.zeros(6), np.array([14.0])])
    derivative = derivative + np.eye(8) * corner_terms[None, :]
    gauss_nodes = np.array(GAUSS_POINTS)
    gauss_weights = np.array(GAUSS_WEIGHTS)
    numerators = gauss_nodes[:, None, None] - gll_nodes[None, None, :]
    denominators = np.where(identity, 1.0, spacing)[None]
    ratios = np.where(identity[None], 1.0, numerators / denominators)
    interpolation = ratios.prod(axis=2)
    slope_interp = interpolation @ derivative
    return derivative, node_weights, interpolation, slope_interp, gauss_weights


def float_tables():
    return tuple(jnp.asarray(member, jnp.float32) for member in node_tables())


def along_first(vector, matrix):
    leading, first_len, second_len, third_len = vector.shape
    columns = matrix.shape[1]
    blocks = vector.reshape(leading, first_len // columns, columns, second_len, third_len)
    result = jnp.einsum("pi,laimz->lapmz", matrix, blocks, precision=HIGH)
    return result.reshape(leading, -1, second_len, third_len)


def along_second(vector, matrix):
    leading, first_len, second_len, third_len = vector.shape
    columns = matrix.shape[1]
    blocks = vector.reshape(leading, first_len, second_len // columns, columns, third_len)
    result = jnp.einsum("pi,lxaiz->lxapz", matrix, blocks, precision=HIGH)
    return result.reshape(leading, first_len, -1, third_len)


def along_third(vector, matrix, group_size):
    leading, first_len, second_len, third_len = vector.shape
    columns = matrix.shape[1]
    kron_table = jnp.kron(jnp.eye(group_size, dtype=jnp.float32), matrix.T)
    blocks = vector.reshape(leading, first_len, second_len, third_len // (group_size * columns), group_size * columns)
    result = jnp.einsum("lxyzk,kq->lxyzq", blocks, kron_table, precision=HIGH)
    return result.reshape(leading, first_len, second_len, -1)


def interpolate(vector, matrix, group_size):
    return along_third(along_second(along_first(vector, matrix), matrix), matrix, group_size)


def weight_grid(weights, extent):
    nodes_per = weights.shape[0]
    first_axis = jnp.tile(weights, extent[0] // nodes_per)
    second_axis = jnp.tile(weights, extent[1] // nodes_per)
    third_axis = jnp.tile(weights, extent[2] // nodes_per)
    return first_axis[:, None, None] * second_axis[None, :, None] * third_axis[None, None, :]


def transposed_operator(vector, velocity_fine, metric_diag, metric_cross, group_size, tables):
    derivative, node_weights, interpolation, slope_interp, gauss_weights = tables
    grad_first = along_first(vector, derivative)
    grad_second = along_second(vector, derivative)
    grad_third = along_third(vector, derivative, group_size)
    scaled = VISCOSITY * weight_grid(node_weights, vector.shape[1:])
    flux_first = scaled * (metric_diag[0] * grad_first + metric_cross[0] * grad_second + metric_cross[1] * grad_third)
    flux_second = scaled * (metric_cross[0] * grad_first + metric_diag[1] * grad_second + metric_cross[2] * grad_third)
    flux_third = scaled * (metric_cross[1] * grad_first + metric_cross[2] * grad_second + metric_diag[2] * grad_third)
    stiffness = along_first(flux_first, derivative.T) + along_second(flux_second, derivative.T) + along_third(flux_third, derivative.T, group_size)
    fine_field = interpolate(vector, interpolation, group_size)
    weighted = fine_field * weight_grid(gauss_weights, fine_field.shape[1:])
    back_first = along_first(along_second(along_third(velocity_fine[0] * weighted, interpolation.T, group_size), interpolation.T), slope_interp.T)
    back_second = along_first(along_second(along_third(velocity_fine[1] * weighted, interpolation.T, group_size), slope_interp.T), interpolation.T)
    back_third = along_first(along_second(along_third(velocity_fine[2] * weighted, slope_interp.T, group_size), interpolation.T), interpolation.T)
    return stiffness + back_first + back_second + back_third


def add_partners(padded, which_axis):
    nodes_along = padded.shape[which_axis] - 2
    middle_part = lax.slice_in_dim(padded, 1, nodes_along + 1, axis=which_axis)
    next_part = lax.slice_in_dim(padded, 2, nodes_along + 2, axis=which_axis)
    before = lax.slice_in_dim(padded, 0, nodes_along, axis=which_axis)
    position = (jnp.arange(nodes_along) % 8).reshape(tuple(nodes_along if dimension == which_axis else 1 for dimension in range(padded.ndim)))
    return middle_part + jnp.where(position == 7, next_part, 0.0) + jnp.where(position == 0, before, 0.0)


def assemble_global(vector):
    section_one = add_partners(jnp.concatenate([vector[:, -1:], vector, vector[:, :1]], axis=1), 1)
    section_two = add_partners(jnp.concatenate([section_one[:, :, -1:], section_one, section_one[:, :, :1]], axis=2), 2)
    padded = jnp.pad(section_two, ((0, 0), (0, 0), (0, 0), (1, 1)))
    return add_partners(padded, 3)


def apply_global(vector, base_flow, metric_diag, metric_cross, tables):
    slab_total = vector.shape[1] // 8

    def one_slab(slab_index):
        offset = slab_index * 8
        pieces = [lax.dynamic_slice_in_dim(member, offset, 8, axis=1) for member in (vector, base_flow, metric_diag, metric_cross)]
        fine_flow = interpolate(pieces[1], tables[2], 1)
        return transposed_operator(pieces[0], fine_flow, pieces[2], pieces[3], 1, tables)

    stacked = lax.map(one_slab, jnp.arange(slab_total, dtype=jnp.int32))
    return jnp.transpose(stacked, (1, 0, 2, 3, 4)).reshape(vector.shape)


def reference(adjoint_field, base_flow, metric_diag, metric_cross, jacobian):
    tables = float_tables()
    first_term = apply_global(adjoint_field, base_flow, metric_diag, metric_cross, tables)
    mass_terms = jacobian * weight_grid(tables[1], jacobian.shape)
    assembled = assemble_global(jnp.concatenate([first_term, mass_terms[None]], axis=0))
    inverse_mass = 1.0 / assembled[3]
    planes = jacobian.shape[2]
    global_plane = jnp.arange(planes)
    interior = ((global_plane > 0) & (global_plane < planes - 1)).astype(jnp.float32)
    half_state = interior * (adjoint_field - (0.5 * STEP_SIZE) * inverse_mass * assembled[:3])
    second_term = assemble_global(apply_global(half_state, base_flow, metric_diag, metric_cross, tables))
    return interior * (adjoint_field - STEP_SIZE * inverse_mass * second_term)
```

```python
import functools

import jax
import jax.numpy as jnp
import numpy as np
from jax import lax
from jax.experimental import pallas as pl
from jax.experimental.pallas import tpu as pltpu
from jax.sharding import PartitionSpec as P

VISCOSITY = 0.05
STEP_SIZE = 0.01
GLL_INNER = [
    -0.8717401485096066,
    -0.5917001814331423,
    -0.2092992179024789,
    0.2092992179024789,
    0.5917001814331423,
    0.8717401485096066,
]
GAUSS_POINTS = [
    -0.9815606342467192,
    -0.9041172563704749,
    -0.7699026741943047,
    -0.5873179542866175,
    -0.3678314989981802,
    -0.1252334085114689,
    0.1252334085114689,
    0.3678314989981802,
    0.5873179542866175,
    0.7699026741943047,
    0.9041172563704749,
    0.9815606342467192,
]
GAUSS_WEIGHTS = [
    0.0471753363865118,
    0.1069393259953184,
    0.1600783285433462,
    0.2031674267230659,
    0.2334925365383548,
    0.2491470458134028,
    0.2491470458134028,
    0.2334925365383548,
    0.2031674267230659,
    0.1600783285433462,
    0.1069393259953184,
    0.0471753363865118,
]
F32 = jnp.float32
BF16 = jnp.bfloat16
XY = 64
QQ = 144
LANES = 128


def legendre_seven(points):
    previous = points * 0.0 + 1.0
    current = points
    for degree in range(1, 7):
        following = ((2.0 * degree + 1.0) * points * current - degree * previous) / (degree + 1.0)
        previous = current
        current = following
    return current


def node_tables():
    gll_nodes = np.array([-1.0] + GLL_INNER + [1.0])
    values = legendre_seven(gll_nodes)
    node_weights = 2.0 / (56.0 * values * values)
    identity = np.eye(8, dtype=bool)
    spacing = gll_nodes[:, None] - gll_nodes[None, :]
    derivative = np.where(
        identity, 0.0, values[:, None] / (values[None, :] * np.where(identity, 1.0, spacing))
    )
    corner_terms = np.concatenate([np.array([-14.0]), np.zeros(6), np.array([14.0])])
    derivative = derivative + np.eye(8) * corner_terms[None, :]
    gauss_nodes = np.array(GAUSS_POINTS)
    gauss_weights = np.array(GAUSS_WEIGHTS)
    numerators = gauss_nodes[:, None, None] - gll_nodes[None, None, :]
    denominators = np.where(identity, 1.0, spacing)[None]
    ratios = np.where(identity[None], 1.0, numerators / denominators)
    interpolation = ratios.prod(axis=2)
    slope_interp = interpolation @ derivative
    return (derivative, node_weights, interpolation, slope_interp, gauss_weights)


def halves(matrix):
    high = np.asarray(matrix, np.float32).astype(jnp.bfloat16)
    low = (np.asarray(matrix, np.float64) - high.astype(np.float64)).astype(jnp.bfloat16)
    return high, low


def constants():
    dm, rho, jm, dj, sigma = node_tables()
    def forward_block(matrix):
        high, low = halves(matrix)
        return np.block([[high, low], [high, np.zeros_like(low)]])

    dz = np.kron(np.eye(16), dm.T)
    jz = np.kron(np.eye(16), jm.T)
    last = np.concatenate([jz[:, LANES:], np.zeros((LANES, 64))], axis=1)
    z_forward = np.concatenate(
        [forward_block(dz), forward_block(jz[:, :LANES]), forward_block(last)], axis=1
    )
    def three(matrix):
        high, low = halves(matrix)
        return np.concatenate([high, high, low], axis=1)

    jj = three(np.kron(jm, jm))
    eye = np.eye(8)
    grads = three(np.concatenate([np.kron(dm, eye), np.kron(eye, dm)], axis=0))
    js, ds = sigma[:, None] * jm, sigma[:, None] * dj

    def stacked(matrix):
        high, low = halves(matrix)
        return np.concatenate(
            [
                np.concatenate([high, high], axis=1),
                np.concatenate([low, np.zeros_like(low)], axis=1),
            ],
            axis=0,
        )

    back_12 = stacked(np.concatenate([np.kron(ds, js).T, np.kron(js, ds).T], axis=1))
    back_3 = stacked(np.kron(js, js).T)
    div = np.concatenate([np.kron(dm.T, eye), np.kron(eye, dm.T)], axis=1)
    div_high, div_low = halves(div)
    div = np.concatenate([div_high, div_high, div_low], axis=1)
    def back_block(matrix):
        padded = np.concatenate([matrix, np.zeros((64, LANES))], axis=0)
        high, low = halves(padded)
        return [
            np.concatenate([high, low], axis=1),
            np.concatenate([high, np.zeros_like(low)], axis=1),
        ]

    jz_back = np.kron(np.eye(16), js)
    dz_back = np.kron(np.eye(16), ds)
    z_back = np.concatenate(
        back_block(jz_back) + back_block(dz_back) + [forward_block(np.kron(np.eye(16), dm))], axis=0
    )
    weights = np.einsum("x,y,z->xyz", rho, rho, np.tile(rho, 16)).reshape(XY, LANES)
    return (
        [z_forward, jj, grads, back_12, back_3, div, z_back],
        np.asarray(weights, np.float32),
    )


def split(values):
    high = values.astype(BF16)
    low = (values - high.astype(F32)).astype(BF16)
    return high, low


def dot(left, right):
    return jnp.dot(left, right, preferred_element_type=F32)


def fold(values):
    return values[:, :LANES] + values[:, LANES : 2 * LANES]


def section_rows(block, e):
    return block.reshape(8, 2, 8, LANES)[:, e].reshape(XY, LANES)


def interpolate_wall(js_ref, first, last):
    for c in range(3):
        rows = slice(c * XY, (c + 1) * XY)
        tiles = [first[0][rows], first[1][rows]]
        tiles.append(last[0][rows] + pltpu.roll(last[1][rows], 64, 1))
        for t, tile in enumerate(tiles):
            lanes = slice((3 * c + t) * LANES, (3 * c + t + 1) * LANES)
            high, low = split(tile)
            js_ref[0:XY, lanes] = high
            js_ref[XY : 2 * XY, lanes] = low
            js_ref[2 * XY : 3 * XY, lanes] = high


def fine_flow(base_ref, tables, scratch, u_ref):
    z_forward, jj = tables[0], tables[1]
    xhl, js = scratch["xhl"], scratch["js"]
    first, last = [], []
    for e in range(2):
        for c in range(3):
            high, low = split(section_rows(base_ref[c], e))
            xhl[e, c * XY : (c + 1) * XY, :LANES] = high
            xhl[e, c * XY : (c + 1) * XY, LANES:] = low
        out = dot(xhl[e], z_forward[:, 2 * LANES :])
        first.append(fold(out[:, : 2 * LANES]))
        last.append(fold(out[:, 2 * LANES :]))
    interpolate_wall(js, first, last)
    for d in range(3):
        lanes = slice(d * 3 * LANES, (d + 1) * 3 * LANES)
        u_ref[:, lanes] = dot(jj[...], js[:, lanes])


def operator(rows_of, u_ref, metric, tables, scratch):
    z_forward, jj, grads, back_12, back_3, div, z_back = tables
    xhl, js, vs, bz, ts, hs = (scratch[k] for k in ("xhl", "js", "vs", "bz", "ts", "hs"))
    gz, first, last = [], [], []
    for e in range(2):
        for c in range(3):
            high, low = split(rows_of(c, e))
            xhl[e, c * XY : (c + 1) * XY, :LANES] = high
            xhl[e, c * XY : (c + 1) * XY, LANES:] = low
            lanes = slice((2 * c + e) * LANES, (2 * c + e + 1) * LANES)
            vs[0:XY, lanes] = high
            vs[XY : 2 * XY, lanes] = low
            vs[2 * XY : 3 * XY, lanes] = high
        out = dot(xhl[e], z_forward[...])
        gz.append(fold(out[:, : 2 * LANES]))
        first.append(fold(out[:, 2 * LANES : 4 * LANES]))
        last.append(fold(out[:, 4 * LANES :]))
    interpolate_wall(js, first, last)
    for c in range(3):
        rows = slice(c * XY, (c + 1) * XY)
        pair = slice(2 * c * LANES, 2 * (c + 1) * LANES)
        gxy = dot(grads[...], vs[:, pair])
        for e in range(2):
            lanes = slice(e * LANES, (e + 1) * LANES)
            g1, g2, g3 = gxy[:XY, lanes], gxy[XY:, lanes], gz[e][rows]
            m11, m22, m33, m12, m13, m23 = (metric[k, e] for k in range(6))
            h1 = m11 * g1 + m12 * g2 + m13 * g3
            h2 = m12 * g1 + m22 * g2 + m23 * g3
            h3 = m13 * g1 + m23 * g2 + m33 * g3
            h1h, h1l = split(h1)
            h2h, h2l = split(h2)
            h3h, h3l = split(h3)
            lanes = slice((2 * c + e) * LANES, (2 * c + e + 1) * LANES)
            for k, part in enumerate((h1h, h2h, h1l, h2l, h1h, h2h)):
                hs[k * XY : (k + 1) * XY, lanes] = part
            bz[e, rows, 8 * LANES : 9 * LANES] = h3h
            bz[e, rows, 9 * LANES :] = h3l
    for c in range(3):
        rows = slice(c * XY, (c + 1) * XY)
        fine = dot(jj[...], js[:, 3 * c * LANES : 3 * (c + 1) * LANES])
        for d in range(3):
            high, low = split(u_ref[:, 3 * d * LANES : 3 * (d + 1) * LANES] * fine)
            start = (0, QQ, 4 * QQ)[d]
            gap = (2 * QQ, 2 * QQ, QQ)[d]
            ts[start : start + QQ, :] = high
            ts[start + gap : start + gap + QQ, :] = low
        for k, (table, where) in enumerate(
            ((back_12, slice(0, 4 * QQ)), (back_3, slice(4 * QQ, 6 * QQ)))
        ):
            both = dot(table[...], ts[where, :])
            both = both[:XY] + both[XY:]
            mixed = both[:, 2 * LANES :]
            for e in range(2):
                near = both[:, e * LANES : (e + 1) * LANES]
                far = mixed if e == 0 else pltpu.roll(mixed, 64, 1)
                for t, tile in enumerate((near, far)):
                    high, low = split(tile)
                    at = (4 * k + t) * LANES
                    bz[e, rows, at : at + LANES] = high
                    bz[e, rows, at + 2 * LANES : at + 3 * LANES] = low
    spread = dot(div[...], hs[...])
    result = [[None, None] for _ in range(3)]
    for e in range(2):
        out = fold(dot(bz[e], z_back[...]))
        for c in range(3):
            lanes = slice((2 * c + e) * LANES, (2 * c + e + 1) * LANES)
            result[c][e] = out[c * XY : (c + 1) * XY] + spread[:, lanes]
    return result


def sum_local(pair, out_ref, slot):
    row = lax.broadcasted_iota(jnp.int32, (8, 8, LANES), 1)
    lane = lax.broadcasted_iota(jnp.int32, (8, 8, LANES), 2)
    inner = lane % 8
    for e in range(2):
        mine = pair[e].reshape(8, 8, LANES)
        other = pair[1 - e].reshape(8, 8, LANES)
        total = mine + jnp.where(row == 7, pltpu.roll(other, 7, 1), 0.0)
        total = total + jnp.where(row == 0, pltpu.roll(other, 1, 1), 0.0)
        after = pltpu.roll(total, LANES - 1, 2)
        before = pltpu.roll(total, 1, 2)
        total = (
            total
            + jnp.where((inner == 7) & (lane < LANES - 1), after, 0.0)
            + jnp.where((inner == 0) & (lane > 0), before, 0.0)
        )
        out_ref[slot, :, 8 * e : 8 * (e + 1), :] = total


def positions():
    s, c = lax.axis_index("span"), lax.axis_index("col")
    return s % 2, c % 2, c == 0, c == lax.axis_size("col") - 1


def send_parts(fields, sum_ref, so_ref, se_ref, edge_ref):
    odd, _, _, _ = positions()
    for slot in range(fields):
        so_ref[slot] = sum_ref[slot, 7 * odd]
        se_ref[slot] = sum_ref[slot, 7 - 7 * odd]
    lane = lax.broadcasted_iota(jnp.int32, (8, LANES), 1)
    packed = jnp.zeros((8, LANES), F32)
    for slot in range(fields):
        for x in range(8):
            for e in range(2):
                at = slot * 16 + x * 2 + e
                tile = sum_ref[slot, x, 8 * e : 8 * (e + 1), :]
                packed = jnp.where(lane == at, pltpu.roll(tile, (at + 1) % LANES, 1), packed)
                packed = jnp.where(lane == 64 + at, pltpu.roll(tile, 64 + at, 1), packed)
    edge_ref[...] = packed


def receive(fields, sum_ref, so_ref, se_ref, edge_refs):
    odd, col_odd, _, _ = positions()
    x_so, x_se = 7 * odd, 7 - 7 * odd
    for slot in range(fields):
        sum_ref[slot, x_so] += so_ref[slot]
        sum_ref[slot, x_se] += se_ref[slot]
    lane = lax.broadcasted_iota(jnp.int32, (8, LANES), 1)
    x_of = (lane % 16) // 2

    def moved(tile, target):
        shifted = jnp.where(target == 7, pltpu.roll(tile, 14, 1), pltpu.roll(tile, LANES - 14, 1))
        return jnp.where(x_of == target, shifted, 0.0)

    total = jnp.zeros((8, LANES), F32)
    for k in range(len(edge_refs) // 3):
        straight, by_so, by_se = (ref[...] for ref in edge_refs[3 * k : 3 * k + 3])
        sent = straight + moved(by_so, x_so) + moved(by_se, x_se)
        sent = pltpu.roll(sent, 64, 1)
        high = (col_odd == 0) if k == 0 else (col_odd == 1)
        total = total + jnp.where((lane < 64) == high, sent, 0.0)
    for slot in range(fields):
        for x in range(8):
            for e in range(2):
                at = slot * 16 + x * 2 + e
                add = jnp.where(lane == LANES - 1, pltpu.roll(total, LANES - 1 - at, 1), 0.0)
                add = jnp.where(lane == 0, pltpu.roll(total, (64 - at) % LANES, 1), add)
                sum_ref[slot, x, 8 * e : 8 * (e + 1), :] += add


def interior_mask():
    _, _, first, last = positions()
    lane = lax.broadcasted_iota(jnp.int32, (1, 1, LANES), 2)
    outer = ((lane == 0) & first) | ((lane == LANES - 1) & last)
    return jnp.where(outer, 0.0, 1.0)


def scale_metric(diag_ref, cross_ref, weights, metric):
    for k in range(6):
        ref = diag_ref if k < 3 else cross_ref
        block = ref[k % 3].astype(F32)
        for e in range(2):
            metric[k, e] = section_rows(block, e) * weights[...] * VISCOSITY


def first_kernel(*refs):
    sources, (v, *tables, u, metric, total, so, se, edge) = refs[:13], refs[13:27]
    local_refs, sems = refs[27:32], refs[32]
    scratch = dict(zip(SCRATCH_NAMES, refs[33:]))
    b, gd, gc, jac, w = local_refs
    targets = [b, tables[0], tables[1], v, gd, gc, w, jac] + tables[2:]
    copies = [
        pltpu.make_async_copy(source, target, sems.at[k])
        for k, (source, target) in enumerate(zip(sources, targets))
    ]
    for copy in copies:
        copy.start()
    for copy in copies[:3]:
        copy.wait()
    fine_flow(b, tables, scratch, u)
    for copy in copies[3:]:
        copy.wait()
    scale_metric(gd, gc, w, metric)
    result = operator(lambda c, e: section_rows(v[c], e), u, metric, tables, scratch)
    for c in range(3):
        sum_local(result[c], total, c)
    sum_local([section_rows(jac[...], e) * w[...] for e in range(2)], total, 3)
    send_parts(4, total, so, se, edge)


def second_kernel(edges, *refs):
    v, *tables = refs[:8]
    u, metric, summed, so_in, se_in = refs[8:13]
    edge_in = refs[13 : 13 + edges]
    inverse, total, so, se, edge = refs[13 + edges : 18 + edges]
    scratch = dict(zip(SCRATCH_NAMES + ["held", "half"], refs[18 + edges :]))
    held, half = scratch["held"], scratch["half"]
    held[...] = summed[...]
    receive(4, held, so_in, se_in, edge_in)
    inner = interior_mask()
    inv = 1.0 / held[3]
    inverse[...] = inv
    for c in range(3):
        half[c] = inner * (v[c] - (0.5 * STEP_SIZE) * inv * held[c])
    result = operator(lambda c, e: section_rows(half[c], e), u, metric, tables, scratch)
    for c in range(3):
        sum_local(result[c], total, c)
    send_parts(3, total, so, se, edge)


def third_kernel(edges, *refs):
    v, inverse, summed, so_in, se_in = refs[:5]
    edge_in = refs[5 : 5 + edges]
    out, held, sems = refs[5 + edges :]
    held[...] = summed[...]
    receive(3, held, so_in, se_in, edge_in)
    inner = interior_mask()
    copies = []
    for c in range(3):
        held[c] = inner * (v[c] - STEP_SIZE * inverse[...] * held[c])
        copies.append(pltpu.make_async_copy(held.at[c], out.at[c], sems.at[c]))
        copies[-1].start()
    for copy in copies:
        copy.wait()


SCRATCH_NAMES = ["xhl", "js", "vs", "bz", "ts", "hs"]


def scratch_shapes():
    return [
        pltpu.VMEM((2, 3 * XY, 2 * LANES), BF16),
        pltpu.VMEM((3 * XY, 9 * LANES), BF16),
        pltpu.VMEM((3 * XY, 6 * LANES), BF16),
        pltpu.VMEM((2, 3 * XY, 10 * LANES), BF16),
        pltpu.VMEM((6 * QQ, 3 * LANES), BF16),
        pltpu.VMEM((6 * XY, 6 * LANES), BF16),
    ]


def call(kernel, name, ins, outs, scratch, in_space=pltpu.VMEM, out_space=pltpu.VMEM):
    ins = [pltpu.with_memory_space_constraint(array, in_space) for array in ins]
    return pl.pallas_call(
        kernel,
        name=name,
        out_shape=[out_space(shape, dtype) for shape, dtype in outs],
        in_specs=[pl.BlockSpec(memory_space=in_space)] * len(ins),
        out_specs=[pl.BlockSpec(memory_space=out_space)] * len(outs),
        scratch_shapes=scratch,
        compiler_params=pltpu.CompilerParams(vmem_limit_bytes=24 * 1024 * 1024),
    )(*ins)


def pairings(count, periodic):
    even = [(i, i + 1) for i in range(0, count - 1, 2)]
    odd = [(i, i + 1) for i in range(1, count - 1, 2)]
    if periodic:
        odd.append((count - 1, 0))
    return [pairs + [(b, a) for a, b in pairs] for pairs in (odd, even)]


def exchange(so, se, edge):
    spans, cols = lax.axis_size("span"), lax.axis_size("col")
    span_odd, span_even = pairings(spans, True)
    col_odd, col_even = pairings(cols, False)
    so_in = lax.ppermute(so, "span", span_odd)
    se_in = lax.ppermute(se, "span", span_even)
    edges = []
    for col_pairs in (col_even, col_odd):
        if not col_pairs:
            continue
        edges.append(lax.ppermute(edge, "col", col_pairs))
        for span_pairs in (span_odd, span_even):
            both = [
                (s * cols + c, t * cols + d) for s, t in span_pairs for c, d in col_pairs
            ]
            edges.append(lax.ppermute(edge, ("span", "col"), both))
    return so_in, se_in, edges


def local(adjoint_field, base_flow, metric_diag, metric_cross, jacobian):
    tables, weights = constants()
    tables = [jnp.asarray(table, BF16) for table in tables]
    weights = jnp.asarray(weights)
    block = adjoint_field.shape[1:]
    plane = block[1:]
    ins = [base_flow, tables[0], tables[1], adjoint_field, metric_diag, metric_cross]
    ins += [weights, jacobian] + tables[2:]
    field = ((3,) + block, F32)
    v, *rest = call(
        first_kernel,
        "first_operator",
        ins,
        [field]
        + [(table.shape, BF16) for table in tables]
        + [((QQ, 9 * LANES), F32), ((6, 2, XY, LANES), F32), ((4,) + block, F32)]
        + [((4,) + plane, F32)] * 2
        + [((8, LANES), F32)],
        [
            pltpu.VMEM((3,) + block, F32),
            pltpu.VMEM((3,) + block, BF16),
            pltpu.VMEM((3,) + block, BF16),
            pltpu.VMEM(block, F32),
            pltpu.VMEM(weights.shape, F32),
            pltpu.SemaphoreType.DMA((len(ins),)),
        ]
        + scratch_shapes(),
        in_space=pltpu.HBM,
    )
    *state, so, se, edge = rest
    so, se, edges = exchange(so, se, edge)
    inverse, total, so, se, edge = call(
        functools.partial(second_kernel, len(edges)),
        "second_operator",
        [v] + state + [so, se] + edges,
        [(block, F32), field] + [((3,) + plane, F32)] * 2 + [((8, LANES), F32)],
        scratch_shapes() + [pltpu.VMEM((4,) + block, F32), pltpu.VMEM((3,) + block, F32)],
    )
    so, se, edges = exchange(so, se, edge)
    (out,) = call(
        functools.partial(third_kernel, len(edges)),
        "advance",
        [v, inverse, total, so, se] + edges,
        [field],
        [pltpu.VMEM((3,) + block, F32), pltpu.SemaphoreType.DMA((3,))],
        out_space=pltpu.HBM,
    )
    return out


def solution(mesh):
    in_specs = (
        P(None, "span", None, "col"),
        P(None, "span", None, "col"),
        P(None, "span", None, "col"),
        P(None, "span", None, "col"),
        P("span", None, "col"),
    )
    out_specs = P(None, "span", None, "col")
    return jax.shard_map(local, mesh=mesh, in_specs=in_specs, out_specs=out_specs, check_vma=False)
```

```python
import functools

import jax
import jax.numpy as jnp
import numpy as np
from jax import lax
from jax.experimental import pallas as pl
from jax.experimental.pallas import tpu as pltpu
from jax.sharding import PartitionSpec as P

VISCOSITY = 0.05
STEP_SIZE = 0.01
GLL_INNER = [
    -0.8717401485096066,
    -0.5917001814331423,
    -0.2092992179024789,
    0.2092992179024789,
    0.5917001814331423,
    0.8717401485096066,
]
GAUSS_POINTS = [
    -0.9815606342467192,
    -0.9041172563704749,
    -0.7699026741943047,
    -0.5873179542866175,
    -0.3678314989981802,
    -0.1252334085114689,
    0.1252334085114689,
    0.3678314989981802,
    0.5873179542866175,
    0.7699026741943047,
    0.9041172563704749,
    0.9815606342467192,
]
GAUSS_WEIGHTS = [
    0.0471753363865118,
    0.1069393259953184,
    0.1600783285433462,
    0.2031674267230659,
    0.2334925365383548,
    0.2491470458134028,
    0.2491470458134028,
    0.2334925365383548,
    0.2031674267230659,
    0.1600783285433462,
    0.1069393259953184,
    0.0471753363865118,
]
F32 = jnp.float32
BF16 = jnp.bfloat16
XY = 64
QQ = 144
LANES = 128


def legendre_seven(points):
    previous = points * 0.0 + 1.0
    current = points
    for degree in range(1, 7):
        following = ((2.0 * degree + 1.0) * points * current - degree * previous) / (degree + 1.0)
        previous = current
        current = following
    return current


def node_tables():
    gll_nodes = np.array([-1.0] + GLL_INNER + [1.0])
    values = legendre_seven(gll_nodes)
    node_weights = 2.0 / (56.0 * values * values)
    identity = np.eye(8, dtype=bool)
    spacing = gll_nodes[:, None] - gll_nodes[None, :]
    derivative = np.where(
        identity, 0.0, values[:, None] / (values[None, :] * np.where(identity, 1.0, spacing))
    )
    corner_terms = np.concatenate([np.array([-14.0]), np.zeros(6), np.array([14.0])])
    derivative = derivative + np.eye(8) * corner_terms[None, :]
    gauss_nodes = np.array(GAUSS_POINTS)
    gauss_weights = np.array(GAUSS_WEIGHTS)
    numerators = gauss_nodes[:, None, None] - gll_nodes[None, None, :]
    denominators = np.where(identity, 1.0, spacing)[None]
    ratios = np.where(identity[None], 1.0, numerators / denominators)
    interpolation = ratios.prod(axis=2)
    slope_interp = interpolation @ derivative
    return (derivative, node_weights, interpolation, slope_interp, gauss_weights)


def halves(matrix):
    high = np.asarray(matrix, np.float32).astype(jnp.bfloat16)
    low = (np.asarray(matrix, np.float64) - high.astype(np.float64)).astype(jnp.bfloat16)
    return high, low


def constants():
    dm, rho, jm, dj, sigma = node_tables()
    def forward_block(matrix):
        high, low = halves(matrix)
        return np.block([[high, low], [high, np.zeros_like(low)]])

    dz = np.kron(np.eye(16), dm.T)
    jz = np.kron(np.eye(16), jm.T)
    last = np.concatenate([jz[:, LANES:], np.zeros((LANES, 64))], axis=1)
    z_forward = np.concatenate(
        [forward_block(dz), forward_block(jz[:, :LANES]), forward_block(last)], axis=1
    )
    def three(matrix):
        high, low = halves(matrix)
        return np.concatenate([high, high, low], axis=1)

    jj = three(np.kron(jm, jm))
    eye = np.eye(8)
    grads = three(np.concatenate([np.kron(dm, eye), np.kron(eye, dm)], axis=0))
    js, ds = sigma[:, None] * jm, sigma[:, None] * dj

    def stacked(matrix):
        high, low = halves(matrix)
        return np.concatenate(
            [
                np.concatenate([high, high], axis=1),
                np.concatenate([low, np.zeros_like(low)], axis=1),
            ],
            axis=0,
        )

    back_12 = stacked(np.concatenate([np.kron(ds, js).T, np.kron(js, ds).T], axis=1))
    back_3 = stacked(np.kron(js, js).T)
    div = np.concatenate([np.kron(dm.T, eye), np.kron(eye, dm.T)], axis=1)
    div_high, div_low = halves(div)
    div = np.concatenate([div_high, div_high, div_low], axis=1)
    def back_block(matrix):
        padded = np.concatenate([matrix, np.zeros((64, LANES))], axis=0)
        high, low = halves(padded)
        return [
            np.concatenate([high, low], axis=1),
            np.concatenate([high, np.zeros_like(low)], axis=1),
        ]

    jz_back = np.kron(np.eye(16), js)
    dz_back = np.kron(np.eye(16), ds)
    z_back = np.concatenate(
        back_block(jz_back) + back_block(dz_back) + [forward_block(np.kron(np.eye(16), dm))], axis=0
    )
    weights = np.einsum("x,y,z->xyz", rho, rho, np.tile(rho, 16)).reshape(XY, LANES)
    return (
        [z_forward, jj, grads, back_12, back_3, div, z_back],
        np.asarray(weights, np.float32),
    )


def split(values):
    high = values.astype(BF16)
    low = (values - high.astype(F32)).astype(BF16)
    return high, low


def dot(left, right):
    return jnp.dot(left, right, preferred_element_type=F32)


def fold(values):
    return values[:, :LANES] + values[:, LANES : 2 * LANES]


def section_rows(block, e):
    return block.reshape(8, 2, 8, LANES)[:, e].reshape(XY, LANES)


def interpolate_wall(js_ref, first, last):
    for c in range(3):
        rows = slice(c * XY, (c + 1) * XY)
        tiles = [first[0][rows], first[1][rows]]
        tiles.append(last[0][rows] + pltpu.roll(last[1][rows], 64, 1))
        for t, tile in enumerate(tiles):
            lanes = slice((3 * c + t) * LANES, (3 * c + t + 1) * LANES)
            high, low = split(tile)
            js_ref[0:XY, lanes] = high
            js_ref[XY : 2 * XY, lanes] = low
            js_ref[2 * XY : 3 * XY, lanes] = high


def fine_flow(base_ref, tables, scratch, u_ref):
    z_forward, jj = tables[0], tables[1]
    xhl, js = scratch["xhl"], scratch["js"]
    first, last = [], []
    for e in range(2):
        for c in range(3):
            high, low = split(section_rows(base_ref[c], e))
            xhl[e, c * XY : (c + 1) * XY, :LANES] = high
            xhl[e, c * XY : (c + 1) * XY, LANES:] = low
        out = dot(xhl[e], z_forward[:, 2 * LANES :])
        first.append(fold(out[:, : 2 * LANES]))
        last.append(fold(out[:, 2 * LANES :]))
    interpolate_wall(js, first, last)
    for d in range(3):
        lanes = slice(d * 3 * LANES, (d + 1) * 3 * LANES)
        u_ref[:, lanes] = dot(jj[...], js[:, lanes])


def operator(rows_of, u_ref, metric, tables, scratch):
    z_forward, jj, grads, back_12, back_3, div, z_back = tables
    xhl, js, vs, bz, ts, hs = (scratch[k] for k in ("xhl", "js", "vs", "bz", "ts", "hs"))
    gz, first, last = [], [], []
    for e in range(2):
        for c in range(3):
            high, low = split(rows_of(c, e))
            xhl[e, c * XY : (c + 1) * XY, :LANES] = high
            xhl[e, c * XY : (c + 1) * XY, LANES:] = low
            lanes = slice((2 * c + e) * LANES, (2 * c + e + 1) * LANES)
            vs[0:XY, lanes] = high
            vs[XY : 2 * XY, lanes] = low
            vs[2 * XY : 3 * XY, lanes] = high
        out = dot(xhl[e], z_forward[...])
        gz.append(fold(out[:, : 2 * LANES]))
        first.append(fold(out[:, 2 * LANES : 4 * LANES]))
        last.append(fold(out[:, 4 * LANES :]))
    interpolate_wall(js, first, last)
    for c in range(3):
        rows = slice(c * XY, (c + 1) * XY)
        pair = slice(2 * c * LANES, 2 * (c + 1) * LANES)
        gxy = dot(grads[...], vs[:, pair])
        for e in range(2):
            lanes = slice(e * LANES, (e + 1) * LANES)
            g1, g2, g3 = gxy[:XY, lanes], gxy[XY:, lanes], gz[e][rows]
            m11, m22, m33, m12, m13, m23 = (metric[k, e] for k in range(6))
            h1 = m11 * g1 + m12 * g2 + m13 * g3
            h2 = m12 * g1 + m22 * g2 + m23 * g3
            h3 = m13 * g1 + m23 * g2 + m33 * g3
            h1h, h1l = split(h1)
            h2h, h2l = split(h2)
            h3h, h3l = split(h3)
            lanes = slice((2 * c + e) * LANES, (2 * c + e + 1) * LANES)
            for k, part in enumerate((h1h, h2h, h1l, h2l, h1h, h2h)):
                hs[k * XY : (k + 1) * XY, lanes] = part
            bz[e, rows, 8 * LANES : 9 * LANES] = h3h
            bz[e, rows, 9 * LANES :] = h3l
    for c in range(3):
        rows = slice(c * XY, (c + 1) * XY)
        fine = dot(jj[...], js[:, 3 * c * LANES : 3 * (c + 1) * LANES])
        for d in range(3):
            high, low = split(u_ref[:, 3 * d * LANES : 3 * (d + 1) * LANES] * fine)
            start = (0, QQ, 4 * QQ)[d]
            gap = (2 * QQ, 2 * QQ, QQ)[d]
            ts[start : start + QQ, :] = high
            ts[start + gap : start + gap + QQ, :] = low
        for k, (table, where) in enumerate(
            ((back_12, slice(0, 4 * QQ)), (back_3, slice(4 * QQ, 6 * QQ)))
        ):
            both = dot(table[...], ts[where, :])
            both = both[:XY] + both[XY:]
            mixed = both[:, 2 * LANES :]
            for e in range(2):
                near = both[:, e * LANES : (e + 1) * LANES]
                far = mixed if e == 0 else pltpu.roll(mixed, 64, 1)
                for t, tile in enumerate((near, far)):
                    high, low = split(tile)
                    at = (4 * k + t) * LANES
                    bz[e, rows, at : at + LANES] = high
                    bz[e, rows, at + 2 * LANES : at + 3 * LANES] = low
    spread = dot(div[...], hs[...])
    result = [[None, None] for _ in range(3)]
    for e in range(2):
        out = fold(dot(bz[e], z_back[...]))
        for c in range(3):
            lanes = slice((2 * c + e) * LANES, (2 * c + e + 1) * LANES)
            result[c][e] = out[c * XY : (c + 1) * XY] + spread[:, lanes]
    return result


def sum_local(pair, out_ref, slot):
    row = lax.broadcasted_iota(jnp.int32, (8, 8, LANES), 1)
    lane = lax.broadcasted_iota(jnp.int32, (8, 8, LANES), 2)
    inner = lane % 8
    for e in range(2):
        mine = pair[e].reshape(8, 8, LANES)
        other = pair[1 - e].reshape(8, 8, LANES)
        total = mine + jnp.where(row == 7, pltpu.roll(other, 7, 1), 0.0)
        total = total + jnp.where(row == 0, pltpu.roll(other, 1, 1), 0.0)
        after = pltpu.roll(total, LANES - 1, 2)
        before = pltpu.roll(total, 1, 2)
        total = (
            total
            + jnp.where((inner == 7) & (lane < LANES - 1), after, 0.0)
            + jnp.where((inner == 0) & (lane > 0), before, 0.0)
        )
        out_ref[slot, :, 8 * e : 8 * (e + 1), :] = total


def positions():
    c = lax.axis_index("col")
    return c % 2, c == 0, c == lax.axis_size("col") - 1


def pack_edges(fields, sum_ref, edge_ref):
    lane = lax.broadcasted_iota(jnp.int32, (8, LANES), 1)
    packed = jnp.zeros((8, LANES), F32)
    for slot in range(fields):
        for x in range(8):
            for e in range(2):
                at = slot * 16 + x * 2 + e
                tile = sum_ref[slot, x, 8 * e : 8 * (e + 1), :]
                packed = jnp.where(lane == at, pltpu.roll(tile, (at + 1) % LANES, 1), packed)
                packed = jnp.where(lane == 64 + at, pltpu.roll(tile, 64 + at, 1), packed)
    edge_ref[...] = packed


def received_edges(edge_refs):
    col_odd, _, _ = positions()
    lane = lax.broadcasted_iota(jnp.int32, (8, LANES), 1)
    total = jnp.zeros((8, LANES), F32)
    for k, ref in enumerate(edge_refs):
        high = (col_odd == 0) if k == 0 else (col_odd == 1)
        total = total + jnp.where((lane < 64) == high, pltpu.roll(ref[...], 64, 1), 0.0)
    return total


def with_edges(tile, edges, at):
    lane = lax.broadcasted_iota(jnp.int32, (8, LANES), 1)
    add = jnp.where(lane == LANES - 1, pltpu.roll(edges, LANES - 1 - at, 1), 0.0)
    return tile + jnp.where(lane == 0, pltpu.roll(edges, (64 - at) % LANES, 1), add)


def planes_kernel(fields, count, *refs):
    summed, edge_refs, (up, down) = refs[0], refs[1 : 1 + count], refs[1 + count :]
    edges = received_edges(edge_refs)
    for x, plane in ((7, up), (0, down)):
        for slot in range(fields):
            for e in range(2):
                rows = slice(8 * e, 8 * (e + 1))
                at = slot * 16 + x * 2 + e
                plane[slot, rows, :] = with_edges(summed[slot, x, rows, :], edges, at)


def receive(fields, sum_ref, up_ref, down_ref, edge_refs):
    edges = received_edges(edge_refs)
    for slot in range(fields):
        for x in range(8):
            for e in range(2):
                rows = slice(8 * e, 8 * (e + 1))
                tile = with_edges(sum_ref[slot, x, rows, :], edges, slot * 16 + x * 2 + e)
                if x == 0:
                    tile += up_ref[slot, rows, :]
                if x == 7:
                    tile += down_ref[slot, rows, :]
                sum_ref[slot, x, rows, :] = tile


def interior_mask():
    _, first, last = positions()
    lane = lax.broadcasted_iota(jnp.int32, (1, 1, LANES), 2)
    outer = ((lane == 0) & first) | ((lane == LANES - 1) & last)
    return jnp.where(outer, 0.0, 1.0)


def scale_metric(diag_ref, cross_ref, weights, metric):
    for k in range(6):
        ref = diag_ref if k < 3 else cross_ref
        block = ref[k % 3].astype(F32)
        for e in range(2):
            metric[k, e] = section_rows(block, e) * weights[...] * VISCOSITY


def first_kernel(*refs):
    sources, (v, *tables, u, metric, total, edge) = refs[:13], refs[13:25]
    local_refs, sems = refs[25:30], refs[30]
    scratch = dict(zip(SCRATCH_NAMES, refs[31:]))
    b, gd, gc, jac, w = local_refs
    targets = [b, tables[0], tables[1], v, gd, gc, w, jac] + tables[2:]
    copies = [
        pltpu.make_async_copy(source, target, sems.at[k])
        for k, (source, target) in enumerate(zip(sources, targets))
    ]
    for copy in copies:
        copy.start()
    for copy in copies[:3]:
        copy.wait()
    fine_flow(b, tables, scratch, u)
    for copy in copies[3:]:
        copy.wait()
    scale_metric(gd, gc, w, metric)
    result = operator(lambda c, e: section_rows(v[c], e), u, metric, tables, scratch)
    for c in range(3):
        sum_local(result[c], total, c)
    sum_local([section_rows(jac[...], e) * w[...] for e in range(2)], total, 3)
    pack_edges(4, total, edge)


def second_kernel(edges, *refs):
    v, *tables = refs[:8]
    u, metric, summed, up_in, down_in = refs[8:13]
    edge_in = refs[13 : 13 + edges]
    inverse, total, edge = refs[13 + edges : 16 + edges]
    scratch = dict(zip(SCRATCH_NAMES + ["held", "half"], refs[16 + edges :]))
    held, half = scratch["held"], scratch["half"]
    held[...] = summed[...]
    receive(4, held, up_in, down_in, edge_in)
    inner = interior_mask()
    inv = 1.0 / held[3]
    inverse[...] = inv
    for c in range(3):
        half[c] = inner * (v[c] - (0.5 * STEP_SIZE) * inv * held[c])
    result = operator(lambda c, e: section_rows(half[c], e), u, metric, tables, scratch)
    for c in range(3):
        sum_local(result[c], total, c)
    pack_edges(3, total, edge)


def third_kernel(edges, *refs):
    v, inverse, summed, up_in, down_in = refs[:5]
    edge_in = refs[5 : 5 + edges]
    out, held, sems = refs[5 + edges :]
    held[...] = summed[...]
    receive(3, held, up_in, down_in, edge_in)
    inner = interior_mask()
    copies = []
    for c in range(3):
        held[c] = inner * (v[c] - STEP_SIZE * inverse[...] * held[c])
        copies.append(pltpu.make_async_copy(held.at[c], out.at[c], sems.at[c]))
        copies[-1].start()
    for copy in copies:
        copy.wait()


SCRATCH_NAMES = ["xhl", "js", "vs", "bz", "ts", "hs"]


def scratch_shapes():
    return [
        pltpu.VMEM((2, 3 * XY, 2 * LANES), BF16),
        pltpu.VMEM((3 * XY, 9 * LANES), BF16),
        pltpu.VMEM((3 * XY, 6 * LANES), BF16),
        pltpu.VMEM((2, 3 * XY, 10 * LANES), BF16),
        pltpu.VMEM((6 * QQ, 3 * LANES), BF16),
        pltpu.VMEM((6 * XY, 6 * LANES), BF16),
    ]


def call(kernel, name, ins, outs, scratch, in_space=pltpu.VMEM, out_space=pltpu.VMEM):
    ins = [pltpu.with_memory_space_constraint(array, in_space) for array in ins]
    return pl.pallas_call(
        kernel,
        name=name,
        out_shape=[out_space(shape, dtype) for shape, dtype in outs],
        in_specs=[pl.BlockSpec(memory_space=in_space)] * len(ins),
        out_specs=[pl.BlockSpec(memory_space=out_space)] * len(outs),
        scratch_shapes=scratch,
        compiler_params=pltpu.CompilerParams(vmem_limit_bytes=24 * 1024 * 1024),
    )(*ins)


def wall_pairings(count):
    even = [(i, i + 1) for i in range(0, count - 1, 2)]
    odd = [(i, i + 1) for i in range(1, count - 1, 2)]
    return [pairs + [(b, a) for a, b in pairs] for pairs in (even, odd) if pairs]


def exchange(fields, total, edge):
    spans = lax.axis_size("span")
    ahead = [(i, (i + 1) % spans) for i in range(spans)]
    back = [(b, a) for a, b in ahead]
    edges = [lax.ppermute(edge, "col", way) for way in wall_pairings(lax.axis_size("col"))]
    plane = ((fields,) + total.shape[2:], F32)
    up, down = call(
        functools.partial(planes_kernel, fields, len(edges)),
        "planes",
        [total] + edges,
        [plane] * 2,
        [],
    )
    return lax.ppermute(up, "span", ahead), lax.ppermute(down, "span", back), edges


def local(adjoint_field, base_flow, metric_diag, metric_cross, jacobian):
    tables, weights = constants()
    tables = [jnp.asarray(table, BF16) for table in tables]
    weights = jnp.asarray(weights)
    block = adjoint_field.shape[1:]
    ins = [base_flow, tables[0], tables[1], adjoint_field, metric_diag, metric_cross]
    ins += [weights, jacobian] + tables[2:]
    field = ((3,) + block, F32)
    v, *rest = call(
        first_kernel,
        "first_operator",
        ins,
        [field]
        + [(table.shape, BF16) for table in tables]
        + [((QQ, 9 * LANES), F32), ((6, 2, XY, LANES), F32), ((4,) + block, F32)]
        + [((8, LANES), F32)],
        [
            pltpu.VMEM((3,) + block, F32),
            pltpu.VMEM((3,) + block, BF16),
            pltpu.VMEM((3,) + block, BF16),
            pltpu.VMEM(block, F32),
            pltpu.VMEM(weights.shape, F32),
            pltpu.SemaphoreType.DMA((len(ins),)),
        ]
        + scratch_shapes(),
        in_space=pltpu.HBM,
    )
    *state, edge = rest
    up, down, edges = exchange(4, state[-1], edge)
    inverse, total, edge = call(
        functools.partial(second_kernel, len(edges)),
        "second_operator",
        [v] + state + [up, down] + edges,
        [(block, F32), field, ((8, LANES), F32)],
        scratch_shapes() + [pltpu.VMEM((4,) + block, F32), pltpu.VMEM((3,) + block, F32)],
    )
    up, down, edges = exchange(3, total, edge)
    (out,) = call(
        functools.partial(third_kernel, len(edges)),
        "advance",
        [v, inverse, total, up, down] + edges,
        [field],
        [pltpu.VMEM((3,) + block, F32), pltpu.SemaphoreType.DMA((3,))],
        out_space=pltpu.HBM,
    )
    return out


def solution(mesh):
    in_specs = (
        P(None, "span", None, "col"),
        P(None, "span", None, "col"),
        P(None, "span", None, "col"),
        P(None, "span", None, "col"),
        P("span", None, "col"),
    )
    out_specs = P(None, "span", None, "col")
    return jax.shard_map(local, mesh=mesh, in_specs=in_specs, out_specs=out_specs, check_vma=False)
```

```python
import functools

import jax
import jax.numpy as jnp
import numpy as np
from jax import lax
from jax.experimental import pallas as pl
from jax.experimental.pallas import tpu as pltpu
from jax.sharding import PartitionSpec as P

VISCOSITY = 0.05
STEP_SIZE = 0.01
GLL_INNER = [
    -0.8717401485096066,
    -0.5917001814331423,
    -0.2092992179024789,
    0.2092992179024789,
    0.5917001814331423,
    0.8717401485096066,
]
GAUSS_POINTS = [
    -0.9815606342467192,
    -0.9041172563704749,
    -0.7699026741943047,
    -0.5873179542866175,
    -0.3678314989981802,
    -0.1252334085114689,
    0.1252334085114689,
    0.3678314989981802,
    0.5873179542866175,
    0.7699026741943047,
    0.9041172563704749,
    0.9815606342467192,
]
GAUSS_WEIGHTS = [
    0.0471753363865118,
    0.1069393259953184,
    0.1600783285433462,
    0.2031674267230659,
    0.2334925365383548,
    0.2491470458134028,
    0.2491470458134028,
    0.2334925365383548,
    0.2031674267230659,
    0.1600783285433462,
    0.1069393259953184,
    0.0471753363865118,
]
F32 = jnp.float32
BF16 = jnp.bfloat16
XY = 64
QQ = 144
LANES = 128
PART_PLANES = ([0, 7], [1, 2, 3, 4, 5, 6])
PART_ROWS = [[8 * x + y for x in planes for y in range(8)] for planes in PART_PLANES]
PAIRS = [(0, 1), (2, 3), (4, 5), (6, 7), (8,)]


def legendre_seven(points):
    previous = points * 0.0 + 1.0
    current = points
    for degree in range(1, 7):
        following = ((2.0 * degree + 1.0) * points * current - degree * previous) / (degree + 1.0)
        previous = current
        current = following
    return current


def node_tables():
    gll_nodes = np.array([-1.0] + GLL_INNER + [1.0])
    values = legendre_seven(gll_nodes)
    node_weights = 2.0 / (56.0 * values * values)
    identity = np.eye(8, dtype=bool)
    spacing = gll_nodes[:, None] - gll_nodes[None, :]
    derivative = np.where(
        identity, 0.0, values[:, None] / (values[None, :] * np.where(identity, 1.0, spacing))
    )
    corner_terms = np.concatenate([np.array([-14.0]), np.zeros(6), np.array([14.0])])
    derivative = derivative + np.eye(8) * corner_terms[None, :]
    gauss_nodes = np.array(GAUSS_POINTS)
    gauss_weights = np.array(GAUSS_WEIGHTS)
    numerators = gauss_nodes[:, None, None] - gll_nodes[None, None, :]
    denominators = np.where(identity, 1.0, spacing)[None]
    ratios = np.where(identity[None], 1.0, numerators / denominators)
    interpolation = ratios.prod(axis=2)
    slope_interp = interpolation @ derivative
    return (derivative, node_weights, interpolation, slope_interp, gauss_weights)


def halves(matrix):
    high = np.asarray(matrix, np.float32).astype(jnp.bfloat16)
    low = (np.asarray(matrix, np.float64) - high.astype(np.float64)).astype(jnp.bfloat16)
    return high, low


def lane_tiles(table):
    rows, columns = table.shape
    padded = np.pad(table, ((0, 0), (0, -columns % LANES)))
    return padded.reshape(rows, -1, LANES).transpose(1, 0, 2)


def constants():
    dm, rho, jm, dj, sigma = node_tables()
    def forward_block(matrix):
        high, low = halves(matrix)
        return np.block([[high, low], [high, np.zeros_like(low)]])

    dz = np.kron(np.eye(16), dm.T)
    jz = np.kron(np.eye(16), jm.T)
    last = np.concatenate([jz[:, LANES:], np.zeros((LANES, 64))], axis=1)
    z_forward = np.concatenate(
        [forward_block(dz), forward_block(jz[:, :LANES]), forward_block(last)], axis=1
    )
    def three(matrix):
        high, low = halves(matrix)
        return np.concatenate([high, high, low], axis=1)

    jj = three(np.kron(jm, jm))
    eye = np.eye(8)
    grads = three(np.concatenate([np.kron(dm, eye), np.kron(eye, dm)], axis=0))
    js, ds = sigma[:, None] * jm, sigma[:, None] * dj

    def stacked(matrix):
        high, low = halves(matrix)
        return np.concatenate(
            [
                np.concatenate([high, high], axis=1),
                np.concatenate([low, np.zeros_like(low)], axis=1),
            ],
            axis=0,
        )

    back_12 = np.concatenate([np.kron(ds, js).T, np.kron(js, ds).T], axis=1)
    back_3 = np.kron(js, js).T
    div = np.concatenate([np.kron(dm.T, eye), np.kron(eye, dm.T)], axis=1)
    by_part = []
    for rows in PART_ROWS:
        by_part += [stacked(back_12[rows]), stacked(back_3[rows]), three(div[rows])]
    def back_block(matrix):
        padded = np.concatenate([matrix, np.zeros((64, LANES))], axis=0)
        high, low = halves(padded)
        return [
            np.concatenate([high, low], axis=1),
            np.concatenate([high, np.zeros_like(low)], axis=1),
        ]

    jz_back = np.kron(np.eye(16), js)
    dz_back = np.kron(np.eye(16), ds)
    z_back = np.concatenate(
        back_block(jz_back) + back_block(dz_back) + [forward_block(np.kron(np.eye(16), dm))], axis=0
    )
    weights = np.einsum("x,y,z->xyz", rho, rho, np.tile(rho, 16)).reshape(XY, LANES)
    return (
        [lane_tiles(t) for t in (z_forward, jj, grads, z_back, *by_part)],
        np.asarray(weights, np.float32),
    )


def split(values):
    high = values.astype(BF16)
    low = (values - high.astype(F32)).astype(BF16)
    return high, low


def dot(left, right):
    return jnp.dot(left, right, preferred_element_type=F32)


def wide(tiles, columns=None):
    whole = jnp.concatenate([tiles[k] for k in range(tiles.shape[0])], axis=1)
    return whole if columns is None else whole[:, :columns]


def fold(values):
    return values[:, :LANES] + values[:, LANES : 2 * LANES]


def section_rows(block, e):
    return block.reshape(8, 2, 8, LANES)[:, e].reshape(XY, LANES)


def interpolate_wall(js_ref, first, last):
    for c in range(3):
        rows = slice(c * XY, (c + 1) * XY)
        tiles = [first[0][rows], first[1][rows]]
        tiles.append(last[0][rows] + pltpu.roll(last[1][rows], 64, 1))
        for t, tile in enumerate(tiles):
            high, low = split(tile)
            js_ref[3 * c + t, 0:XY] = high
            js_ref[3 * c + t, XY : 2 * XY] = low
            js_ref[3 * c + t, 2 * XY : 3 * XY] = high


def tiles_at(ref, tiles, rows=slice(None)):
    return jnp.concatenate([ref[k, rows] for k in tiles], axis=1)


def columns(values, count):
    return [values[:, k * LANES : (k + 1) * LANES] for k in range(count)]


def fine_flow(base_ref, tables, scratch, u_ref):
    z_forward, jj = tables[0], tables[1]
    xhl, js = scratch["xhl"], scratch["js"]
    first, last = [], []
    for e in range(2):
        for c in range(3):
            rows = slice(c * XY, (c + 1) * XY)
            xhl[e, 0, rows], xhl[e, 1, rows] = split(section_rows(base_ref[c], e))
        out = dot(wide(xhl.at[e]), wide(z_forward.at[2:]))
        first.append(fold(out[:, : 2 * LANES]))
        last.append(fold(out[:, 2 * LANES :]))
    interpolate_wall(js, first, last)
    for pair in PAIRS:
        out = dot(wide(jj, 3 * XY), tiles_at(js, pair))
        for k, tile in zip(pair, columns(out, len(pair))):
            u_ref[k] = tile


def front(rows_of, u_ref, metric, tables, scratch, kept):
    z_forward, jj, grads = tables[:3]
    xhl, js, vs = (scratch[k] for k in ("xhl", "js", "vs"))
    ts, hs, h3s = kept
    gz, first, last = [], [], []
    for e in range(2):
        for c in range(3):
            rows = slice(c * XY, (c + 1) * XY)
            high, low = split(rows_of(c, e))
            xhl[e, 0, rows], xhl[e, 1, rows] = high, low
            vs[2 * c + e, 0:XY] = high
            vs[2 * c + e, XY : 2 * XY] = low
            vs[2 * c + e, 2 * XY : 3 * XY] = high
        out = dot(wide(xhl.at[e]), wide(z_forward))
        gz.append(fold(out[:, : 2 * LANES]))
        first.append(fold(out[:, 2 * LANES : 4 * LANES]))
        last.append(fold(out[:, 4 * LANES :]))
    interpolate_wall(js, first, last)

    def flux(c):
        rows = slice(c * XY, (c + 1) * XY)
        gxy = dot(wide(grads, 3 * XY), tiles_at(vs, (2 * c, 2 * c + 1)))
        for e in range(2):
            lanes = slice(e * LANES, (e + 1) * LANES)
            g1, g2, g3 = gxy[:XY, lanes], gxy[XY:, lanes], gz[e][rows]
            m11, m22, m33, m12, m13, m23 = (metric[k, e] for k in range(6))
            h1 = m11 * g1 + m12 * g2 + m13 * g3
            h2 = m12 * g1 + m22 * g2 + m23 * g3
            h3 = m13 * g1 + m23 * g2 + m33 * g3
            h1h, h1l = split(h1)
            h2h, h2l = split(h2)
            for k, part in enumerate((h1h, h2h, h1l, h2l, h1h, h2h)):
                hs[2 * c + e, k * XY : (k + 1) * XY] = part
            h3s[2 * c + e] = h3

    def gauss(pair):
        fine = dot(wide(jj, 3 * XY), tiles_at(js, pair))
        for k, tile in zip(pair, columns(fine, len(pair))):
            for d in range(3):
                start = (0, QQ, 4 * QQ)[d]
                gap = (2 * QQ, 2 * QQ, QQ)[d]
                high, low = split(u_ref[3 * d + k % 3] * tile)
                ts[k, start : start + QQ] = high
                ts[k, start + gap : start + gap + QQ] = low

    gauss(PAIRS[0])
    flux(0)
    gauss(PAIRS[1])
    flux(1)
    gauss(PAIRS[2])
    flux(2)
    gauss(PAIRS[3])
    gauss(PAIRS[4])


def back(part, tables, scratch, kept):
    z_back, back_12, back_3, div = tables
    ts, hs, h3s = kept
    bz = scratch["bz"]
    planes = PART_PLANES[part]
    count = 8 * len(planes)
    result = [[None, None] for _ in range(3)]
    sides = [{}, {}]
    for pair in PAIRS:
        for k, (table, depth, where) in enumerate(
            ((back_12, 4 * QQ, slice(0, 4 * QQ)), (back_3, 2 * QQ, slice(4 * QQ, None)))
        ):
            both = dot(wide(table, depth), tiles_at(ts, pair, where))
            both = both[:count] + both[count:]
            for tile, values in zip(pair, columns(both, len(pair))):
                sides[k][tile] = values
    for c in range(3):
        spread = columns(dot(wide(div), tiles_at(hs, (2 * c, 2 * c + 1))), 2)
        for e in range(2):
            result[c][e] = spread[e]
            rows = slice((2 * c + e) * count, (2 * c + e + 1) * count)
            for k in range(2):
                far = sides[k][3 * c + 2]
                far = far if e == 0 else pltpu.roll(far, 64, 1)
                for t, tile in enumerate((sides[k][3 * c + e], far)):
                    bz[4 * k + t, rows], bz[4 * k + t + 2, rows] = split(tile)
            bz[8, rows], bz[9, rows] = split(part_rows(part, h3s[2 * c + e]))
    out = fold(dot(wide(bz), wide(z_back)))
    for c in range(3):
        for e in range(2):
            result[c][e] += out[(2 * c + e) * count : (2 * c + e + 1) * count]
    return result


def part_rows(part, tall):
    return jnp.concatenate([tall[8 * x : 8 * x + 8] for x in PART_PLANES[part]], axis=0)


def sum_local(pair, out_ref, slot):
    shape = (out_ref.shape[1], 8, LANES)
    row = lax.broadcasted_iota(jnp.int32, shape, 1)
    lane = lax.broadcasted_iota(jnp.int32, shape, 2)
    inner = lane % 8
    for e in range(2):
        mine = pair[e].reshape(shape)
        other = pair[1 - e].reshape(shape)
        total = mine + jnp.where(row == 7, pltpu.roll(other, 7, 1), 0.0)
        total = total + jnp.where(row == 0, pltpu.roll(other, 1, 1), 0.0)
        after = pltpu.roll(total, LANES - 1, 2)
        before = pltpu.roll(total, 1, 2)
        total = (
            total
            + jnp.where((inner == 7) & (lane < LANES - 1), after, 0.0)
            + jnp.where((inner == 0) & (lane > 0), before, 0.0)
        )
        out_ref[slot, :, 8 * e : 8 * (e + 1), :] = total


def positions():
    c = lax.axis_index("col")
    return c % 2, c == 0, c == lax.axis_size("col") - 1


def places(ref):
    fields, planes = ref.shape[:2]
    return [
        (slot, x, e, (slot * planes + x) * 2 + e)
        for slot in range(fields)
        for x in range(planes)
        for e in range(2)
    ]


def pack_edges(sum_ref, edge_ref):
    lane = lax.broadcasted_iota(jnp.int32, (8, LANES), 1)
    packed = jnp.zeros((8, LANES), F32)
    for slot, x, e, at in places(sum_ref):
        tile = sum_ref[slot, x, 8 * e : 8 * (e + 1), :]
        packed = jnp.where(lane == at, pltpu.roll(tile, (at + 1) % LANES, 1), packed)
        packed = jnp.where(lane == 64 + at, pltpu.roll(tile, 64 + at, 1), packed)
    edge_ref[...] = packed


def received_edges(edge_refs):
    col_odd, _, _ = positions()
    lane = lax.broadcasted_iota(jnp.int32, (8, LANES), 1)
    total = jnp.zeros((8, LANES), F32)
    for k, ref in enumerate(edge_refs):
        high = (col_odd == 0) if k == 0 else (col_odd == 1)
        total = total + jnp.where((lane < 64) == high, pltpu.roll(ref[...], 64, 1), 0.0)
    return total


def with_edges(sum_ref, edge_refs):
    edges = received_edges(edge_refs)
    lane = lax.broadcasted_iota(jnp.int32, (8, LANES), 1)
    tiles = {}
    for slot, x, e, at in places(sum_ref):
        add = jnp.where(lane == LANES - 1, pltpu.roll(edges, LANES - 1 - at, 1), 0.0)
        add = jnp.where(lane == 0, pltpu.roll(edges, (64 - at) % LANES, 1), add)
        tiles[slot, x, e] = sum_ref[slot, x, 8 * e : 8 * (e + 1), :] + add
    return tiles


def planes_kernel(count, *refs):
    outer, edge_refs, (up, down) = refs[0], refs[1 : 1 + count], refs[-2:]
    for (slot, x, e), tile in with_edges(outer, edge_refs).items():
        (up if x else down)[slot, 8 * e : 8 * (e + 1), :] = tile


def arrived(outer_ref, edge_refs, up_ref, down_ref):
    tiles = with_edges(outer_ref, edge_refs)
    for slot, x, e in tiles:
        tiles[slot, x, e] += (down_ref if x else up_ref)[slot, 8 * e : 8 * (e + 1), :]
    return tiles


def interior_mask():
    _, first, last = positions()
    lane = lax.broadcasted_iota(jnp.int32, (1, LANES), 1)
    outer = ((lane == 0) & first) | ((lane == LANES - 1) & last)
    return jnp.where(outer, 0.0, 1.0)


def scale_metric(diag_ref, cross_ref, weights, metric):
    for k in range(6):
        ref = diag_ref if k < 3 else cross_ref
        block = ref[k % 3].astype(F32)
        for e in range(2):
            metric[k, e] = section_rows(block, e) * weights[...] * VISCOSITY


def finish(part, kept, tables, scratch, total, edge, mass=None):
    result = back(part, tables, scratch, kept)
    for c in range(3):
        sum_local(result[c], total, c)
    if mass is not None:
        jac, w = mass
        rows = [part_rows(part, section_rows(jac[...], e) * w[...]) for e in range(2)]
        sum_local(rows, total, 3)
    pack_edges(total, edge)


def first_kernel(*refs):
    sources, refs = refs[:16], refs[16:]
    v, tables, (jac, w, u, metric, *kept) = refs[0], refs[1:11], refs[11:18]
    total, edge, b, gd, gc, sems = refs[18:24]
    scratch = dict(zip(SCRATCH_NAMES, refs[24:]))
    targets = [b, tables[0], tables[1], v, gd, gc, w, jac, *tables[2:]]
    copies = [
        pltpu.make_async_copy(source, target, sems.at[k])
        for k, (source, target) in enumerate(zip(sources, targets))
    ]
    for copy in copies:
        copy.start()
    for copy in copies[:3]:
        copy.wait()
    fine_flow(b, tables, scratch, u)
    for copy in copies[3:]:
        copy.wait()
    scale_metric(gd, gc, w, metric)
    front(lambda c, e: section_rows(v[c], e), u, metric, tables, scratch, kept)
    finish(0, kept, tables[3:7], scratch, total, edge, (jac, w))


def inner_kernel(has_mass, *refs):
    kept, tables, refs = refs[:3], refs[3:7], refs[7:]
    mass, refs = (refs[:2], refs[2:]) if has_mass else (None, refs)
    total, edge, *rest = refs
    finish(1, kept, tables, dict(zip(SCRATCH_NAMES, rest)), total, edge, mass)


def second_kernel(edges, *refs):
    v, tables, (u, metric) = refs[0], refs[1:8], refs[8:10]
    outer, inner_sum, up_in, down_in = refs[10:14]
    outer_edges, inner_edges, refs = (
        refs[14 : 14 + edges],
        refs[14 + edges : 14 + 2 * edges],
        refs[14 + 2 * edges :],
    )
    inverse, kept, (total, edge) = refs[0], refs[1:4], refs[4:6]
    scratch = dict(zip(SCRATCH_NAMES + ["half"], refs[6:]))
    half = scratch["half"]
    mask = interior_mask()
    for part, tiles in enumerate(
        (arrived(outer, outer_edges, up_in, down_in), with_edges(inner_sum, inner_edges))
    ):
        for k, x in enumerate(PART_PLANES[part]):
            for e in range(2):
                rows = slice(8 * e, 8 * (e + 1))
                inv = 1.0 / tiles[3, k, e]
                inverse[x, rows] = inv
                for c in range(3):
                    step = (0.5 * STEP_SIZE) * inv * tiles[c, k, e]
                    half[c, x, rows] = mask * (v[c, x, rows] - step)
    front(lambda c, e: section_rows(half[c], e), u, metric, tables, scratch, kept)
    finish(0, kept, tables[3:7], scratch, total, edge)


def advance_kernel(edges, *refs):
    v, inverse, outer, inner_sum, up_in, down_in = refs[:6]
    outer_edges, inner_edges = refs[6 : 6 + edges], refs[6 + edges : 6 + 2 * edges]
    out, held, sems = refs[6 + 2 * edges :]
    mask = interior_mask()
    inner, outermost = with_edges(inner_sum, inner_edges), arrived(outer, outer_edges, up_in, down_in)
    copies = []
    for c in range(3):
        for part, tiles in enumerate((outermost, inner)):
            for k, x in enumerate(PART_PLANES[part]):
                for e in range(2):
                    rows = slice(8 * e, 8 * (e + 1))
                    step = STEP_SIZE * inverse[x, rows] * tiles[c, k, e]
                    held[c, x, rows] = mask * (v[c, x, rows] - step)
        copies.append(pltpu.make_async_copy(held.at[c], out.at[c], sems.at[c]))
        copies[-1].start()
    for copy in copies:
        copy.wait()


SCRATCH_NAMES = ["bz", "xhl", "js", "vs"]


def scratch_shapes(part=None):
    bz = pltpu.VMEM((10, 6 * 8 * len(PART_PLANES[part]), LANES), BF16)
    front_scratch = [
        pltpu.VMEM((2, 2, 3 * XY, LANES), BF16),
        pltpu.VMEM((9, 3 * XY, LANES), BF16),
        pltpu.VMEM((6, 3 * XY, LANES), BF16),
    ]
    return [bz] + (front_scratch if part == 0 else [])


def call(kernel, name, ins, outs, scratch, in_space=pltpu.VMEM, out_space=pltpu.VMEM):
    ins = [pltpu.with_memory_space_constraint(array, in_space) for array in ins]
    return pl.pallas_call(
        kernel,
        name=name,
        out_shape=[out_space(shape, dtype) for shape, dtype in outs],
        in_specs=[pl.BlockSpec(memory_space=in_space)] * len(ins),
        out_specs=[pl.BlockSpec(memory_space=out_space)] * len(outs),
        scratch_shapes=scratch,
        compiler_params=pltpu.CompilerParams(vmem_limit_bytes=24 * 1024 * 1024),
    )(*ins)


def wall_pairings(count):
    even = [(i, i + 1) for i in range(0, count - 1, 2)]
    odd = [(i, i + 1) for i in range(1, count - 1, 2)]
    return [pairs + [(b, a) for a, b in pairs] for pairs in (even, odd) if pairs]


def swap_edges(edge):
    return [lax.ppermute(edge, "col", way) for way in wall_pairings(lax.axis_size("col"))]


def local(adjoint_field, base_flow, metric_diag, metric_cross, jacobian):
    tables, weights = constants()
    tables = [jnp.asarray(table, BF16) for table in tables]
    weights = jnp.asarray(weights)
    block = adjoint_field.shape[1:]
    field = ((3,) + block, F32)
    kept_shapes = [
        ((9, 6 * QQ, LANES), BF16),
        ((6, 6 * XY, LANES), BF16),
        ((6, XY, LANES), F32),
    ]
    edge_shape = ((8, LANES), F32)
    spans = lax.axis_size("span")
    ahead = [(i, (i + 1) % spans) for i in range(spans)]
    back_way = [(b, a) for a, b in ahead]

    def sums(fields, part):
        return [((fields, len(PART_PLANES[part])) + block[1:], F32), edge_shape]

    def exchange(fields, outer, outer_edge, kept, late_tables, mass):
        outer_edges = swap_edges(outer_edge)
        inner, inner_edge = call(
            functools.partial(inner_kernel, len(mass) > 0),
            "inner_planes",
            kept + late_tables + mass,
            sums(fields, 1),
            scratch_shapes(1),
        )
        up, down = call(
            functools.partial(planes_kernel, len(outer_edges)),
            "planes",
            [outer] + outer_edges + [inner_edge],
            [((fields,) + block[1:], F32)] * 2,
            [],
        )
        inner_edges = swap_edges(inner_edge)
        up, down = lax.ppermute(up, "span", ahead), lax.ppermute(down, "span", back_way)
        return up, down, outer_edges, inner, inner_edges

    ins = [base_flow, tables[0], tables[1], adjoint_field, metric_diag, metric_cross]
    ins += [weights, jacobian] + tables[2:]
    out = call(
        first_kernel,
        "first_operator",
        ins,
        [field]
        + [(table.shape, BF16) for table in tables]
        + [(block, F32), (weights.shape, F32)]
        + [((9, QQ, LANES), F32), ((6, 2, XY, LANES), F32)]
        + kept_shapes
        + sums(4, 0),
        [
            pltpu.VMEM((3,) + block, F32),
            pltpu.VMEM((3,) + block, BF16),
            pltpu.VMEM((3,) + block, BF16),
            pltpu.SemaphoreType.DMA((len(ins),)),
        ]
        + scratch_shapes(0),
        in_space=pltpu.HBM,
    )
    v, tables, (jac, w, u, metric), kept = out[0], out[1:11], out[11:15], out[15:18]
    tables, kept = list(tables), list(kept)
    outer, outer_edge = out[18:]
    late_tables = [tables[3]] + tables[7:10]
    up, down, outer_edges, inner, inner_edges = exchange(
        4, outer, outer_edge, kept, late_tables, [jac, w]
    )
    inverse, *kept, outer, outer_edge = call(
        functools.partial(second_kernel, len(outer_edges)),
        "second_operator",
        [v] + tables[:7] + [u, metric, outer, inner, up, down] + outer_edges + inner_edges,
        [(block, F32)] + kept_shapes + sums(3, 0),
        scratch_shapes(0) + [pltpu.VMEM((3,) + block, F32)],
    )
    up, down, outer_edges, inner, inner_edges = exchange(
        3, outer, outer_edge, kept, late_tables, []
    )
    (out,) = call(
        functools.partial(advance_kernel, len(outer_edges)),
        "advance",
        [v, inverse, outer, inner, up, down] + outer_edges + inner_edges,
        [field],
        [pltpu.VMEM((3,) + block, F32), pltpu.SemaphoreType.DMA((3,))],
        out_space=pltpu.HBM,
    )
    return out


def solution(mesh):
    in_specs = (
        P(None, "span", None, "col"),
        P(None, "span", None, "col"),
        P(None, "span", None, "col"),
        P(None, "span", None, "col"),
        P("span", None, "col"),
    )
    out_specs = P(None, "span", None, "col")
    return jax.shard_map(local, mesh=mesh, in_specs=in_specs, out_specs=out_specs, check_vma=False)
```

```python
import functools

import jax
import jax.numpy as jnp
import numpy as np
from jax import lax
from jax.experimental import pallas as pl
from jax.experimental.pallas import tpu as pltpu
from jax.sharding import PartitionSpec as P

VISCOSITY = 0.05
STEP_SIZE = 0.01
GLL_INNER = [
    -0.8717401485096066,
    -0.5917001814331423,
    -0.2092992179024789,
    0.2092992179024789,
    0.5917001814331423,
    0.8717401485096066,
]
GAUSS_POINTS = [
    -0.9815606342467192,
    -0.9041172563704749,
    -0.7699026741943047,
    -0.5873179542866175,
    -0.3678314989981802,
    -0.1252334085114689,
    0.1252334085114689,
    0.3678314989981802,
    0.5873179542866175,
    0.7699026741943047,
    0.9041172563704749,
    0.9815606342467192,
]
GAUSS_WEIGHTS = [
    0.0471753363865118,
    0.1069393259953184,
    0.1600783285433462,
    0.2031674267230659,
    0.2334925365383548,
    0.2491470458134028,
    0.2491470458134028,
    0.2334925365383548,
    0.2031674267230659,
    0.1600783285433462,
    0.1069393259953184,
    0.0471753363865118,
]
F32 = jnp.float32
BF16 = jnp.bfloat16
XY = 64
QQ = 144
LANES = 128
PART_PLANES = ([0, 7], [1, 2, 3, 4, 5, 6])
PART_ROWS = [[8 * x + y for x in planes for y in range(8)] for planes in PART_PLANES]
PAIRS = [(0, 1), (2, 3), (4, 5), (6, 7), (8,)]


def legendre_seven(points):
    previous = points * 0.0 + 1.0
    current = points
    for degree in range(1, 7):
        following = ((2.0 * degree + 1.0) * points * current - degree * previous) / (degree + 1.0)
        previous = current
        current = following
    return current


def node_tables():
    gll_nodes = np.array([-1.0] + GLL_INNER + [1.0])
    values = legendre_seven(gll_nodes)
    node_weights = 2.0 / (56.0 * values * values)
    identity = np.eye(8, dtype=bool)
    spacing = gll_nodes[:, None] - gll_nodes[None, :]
    derivative = np.where(
        identity, 0.0, values[:, None] / (values[None, :] * np.where(identity, 1.0, spacing))
    )
    corner_terms = np.concatenate([np.array([-14.0]), np.zeros(6), np.array([14.0])])
    derivative = derivative + np.eye(8) * corner_terms[None, :]
    gauss_nodes = np.array(GAUSS_POINTS)
    gauss_weights = np.array(GAUSS_WEIGHTS)
    numerators = gauss_nodes[:, None, None] - gll_nodes[None, None, :]
    denominators = np.where(identity, 1.0, spacing)[None]
    ratios = np.where(identity[None], 1.0, numerators / denominators)
    interpolation = ratios.prod(axis=2)
    slope_interp = interpolation @ derivative
    return (derivative, node_weights, interpolation, slope_interp, gauss_weights)


def halves(matrix):
    high = np.asarray(matrix, np.float32).astype(jnp.bfloat16)
    low = (np.asarray(matrix, np.float64) - high.astype(np.float64)).astype(jnp.bfloat16)
    return high, low


def lane_tiles(table):
    rows, columns = table.shape
    padded = np.pad(table, ((0, 0), (0, -columns % LANES)))
    return padded.reshape(rows, -1, LANES).transpose(1, 0, 2)


def three(matrix):
    high, low = halves(matrix)
    return np.concatenate([high, high, low], axis=1)


def stacked(matrix):
    high, low = halves(matrix)
    upper = np.concatenate([high, high], axis=1)
    return np.concatenate([upper, np.concatenate([low, np.zeros_like(low)], axis=1)], axis=0)


def section_tables():
    dm, _, jm, dj, sigma = node_tables()
    eye = np.eye(8)
    values = np.kron(jm, jm)
    slopes = np.concatenate([np.kron(dm, eye), np.kron(eye, dm)], axis=0)
    js, ds = sigma[:, None] * jm, sigma[:, None] * dj
    back_12 = np.concatenate([np.kron(ds, js).T, np.kron(js, ds).T], axis=1)
    back_3 = np.kron(js, js).T
    div = np.concatenate([np.kron(dm.T, eye), np.kron(eye, dm.T)], axis=1)
    tables = {"values": three(values), "slopes": three(slopes)}
    for part, rows in enumerate(PART_ROWS):
        tables["back_12", part] = stacked(back_12[rows])
        tables["back_3", part] = stacked(back_3[rows])
        tables["div", part] = three(div[rows])
        tables["values", part] = three(values[:, rows])
        tables["slopes", part] = three(slopes[:, rows])
    return {name: lane_tiles(table) for name, table in tables.items()}


EARLY = ["values", "slopes", ("back_12", 0), ("back_3", 0), ("div", 0)]
LATE = [("back_12", 1), ("back_3", 1), ("div", 1)]
LATE += [(kind, part) for part in range(2) for kind in ("values", "slopes")]


class Packed:
    def __init__(self, names):
        tables = section_tables()
        self.array = np.concatenate([tables[name].reshape(-1, LANES) for name in names])
        self.places, start = {}, 0
        for name in names:
            self.places[name] = (start, tables[name].shape)
            start += tables[name].shape[0] * tables[name].shape[1]

    def get(self, ref, name):
        start, (tiles, rows, _) = self.places[name]
        return [ref[start + k * rows : start + (k + 1) * rows] for k in range(tiles)]


def wall_bases():
    dm, rho, jm, dj, sigma = node_tables()
    lane = np.arange(LANES)
    gauss = np.arange(24)
    forward_lanes = [lane % 12, (lane + LANES) % 12]
    blocks = [dm.T[:, lane % 8]]
    blocks += [jm.T[:, lanes] for lanes in forward_lanes]
    blocks[2] = np.where(lane < 64, blocks[2], 0.0)
    blocks += [(sigma[:, None] * matrix)[gauss % 12][:, lane % 8] for matrix in (jm, dj)]
    blocks += [dm[:, lane % 8]]
    rows = [np.asarray(part, np.float32) for block in blocks for part in halves(block)]
    rows.append(np.asarray(rho[:, None] * rho[None, lane % 8], np.float32))
    return np.concatenate(rows), [float(weight) for weight in rho]


def build_wall_tables(bases, z_forward, z_back, w, rho):
    row = lax.broadcasted_iota(jnp.int32, (8, LANES), 0)
    lane = lax.broadcasted_iota(jnp.int32, (8, LANES), 1)
    zero = jnp.zeros((8, LANES), F32)
    nothing = jnp.zeros((LANES, LANES), BF16)
    for t in range(6):
        kind, low = t // 2, t % 2
        element = (lane // 8, lane // 12, (lane + LANES) // 12)[kind]
        base = bases[8 * t : 8 * t + 8]
        table = [jnp.where(element == a, base, zero) for a in range(16)]
        table = jnp.concatenate(table, axis=0).astype(BF16)
        z_forward[t, :LANES] = table
        z_forward[t, LANES:] = nothing if low else table
    for kind in range(2):
        for low in range(2):
            start = 48 + 24 * (2 * kind + low)
            table = []
            for block in range(24):
                inside = row + 8 * block - 12 * (lane // 8)
                base = bases[start + 8 * (block % 3) : start + 8 * (block % 3) + 8]
                table.append(jnp.where((inside >= 0) & (inside < 12), base, zero))
            table = jnp.concatenate(table + [zero] * 8, axis=0).astype(BF16)
            z_back[low, 512 * kind : 512 * kind + 256] = table
            z_back[low, 512 * kind + 256 : 512 * (kind + 1)] = (
                jnp.zeros((256, LANES), BF16) if low else table
            )
    for low in range(2):
        base = bases[144 + 8 * low : 152 + 8 * low]
        table = [jnp.where(lane // 8 == a, base, zero) for a in range(16)]
        table = jnp.concatenate(table, axis=0).astype(BF16)
        z_back[low, 1024:1152] = table
        z_back[low, 1152:] = nothing if low else table
    for x in range(8):
        w[8 * x : 8 * x + 8] = bases[160:168] * rho[x]


def split(values):
    high = values.astype(BF16)
    low = (values - high.astype(F32)).astype(BF16)
    return high, low


def dot(left, right):
    return jnp.dot(left, right, preferred_element_type=F32)


def wide(tiles, columns=None):
    count = len(tiles) if isinstance(tiles, list) else tiles.shape[0]
    whole = jnp.concatenate([tiles[k] for k in range(count)], axis=1)
    return whole if columns is None else whole[:, :columns]


def fold(values):
    return values[:, :LANES] + values[:, LANES : 2 * LANES]


def section_rows(block, e):
    return block.reshape(8, 2, 8, LANES)[:, e].reshape(XY, LANES)


def tiles_at(ref, tiles, rows=slice(None)):
    return jnp.concatenate([ref[k, rows] for k in tiles], axis=1)


def columns(values, count):
    return [values[:, k * LANES : (k + 1) * LANES] for k in range(count)]


def wall_stage(rows_of, z_forward, xhl, js, vs=None):
    count = js.shape[1] // 3
    skip = 2 if vs is None else 0
    outs = []
    for e in range(2):
        for c in range(3):
            rows = slice(c * count, (c + 1) * count)
            high, low = split(rows_of(c, e))
            xhl[e, 0, rows], xhl[e, 1, rows] = high, low
            if vs is not None:
                for k, part in enumerate((high, low, high)):
                    vs[2 * c + e, k * count : (k + 1) * count] = part
        outs.append(dot(wide(xhl.at[e]), wide(z_forward.at[skip:])))
    skip = (2 - skip) * LANES
    for c in range(3):
        rows = slice(c * count, (c + 1) * count)
        first = [fold(out[rows, skip : skip + 2 * LANES]) for out in outs]
        last = [fold(out[rows, skip + 2 * LANES :]) for out in outs]
        tiles = first + [last[0] + pltpu.roll(last[1], 64, 1)]
        for t, tile in enumerate(tiles):
            high, low = split(tile)
            for k, part in enumerate((high, low, high)):
                js[3 * c + t, k * count : (k + 1) * count] = part
    if vs is None:
        return None
    return {
        (c, e): fold(outs[e][c * count : (c + 1) * count, : 2 * LANES])
        for c in range(3)
        for e in range(2)
    }


def at_gauss(jj, js, pair):
    depth = js.shape[1]
    return columns(dot(wide(jj, depth), tiles_at(js, pair)), len(pair))


def section_slopes(grads, vs, c):
    return columns(dot(wide(grads, vs.shape[1]), tiles_at(vs, (2 * c, 2 * c + 1))), 2)


def fine_flow(jj, js, u_ref):
    for pair in PAIRS:
        for k, tile in zip(pair, at_gauss(jj, js, pair)):
            u_ref[k] = tile


def front(slopes, jj, grads, js, vs, u_ref, metric, kept, partial=None):
    ts, hs, h3s = kept

    def flux(c):
        for e, both in enumerate(section_slopes(grads, vs, c)):
            if partial is not None:
                both = both + partial[1][2 * c + e]
            g1, g2, g3 = both[:XY], both[XY:], slopes[c, e]
            m11, m22, m33, m12, m13, m23 = (metric[k, e] for k in range(6))
            h1 = m11 * g1 + m12 * g2 + m13 * g3
            h2 = m12 * g1 + m22 * g2 + m23 * g3
            h3 = m13 * g1 + m23 * g2 + m33 * g3
            h1h, h1l = split(h1)
            h2h, h2l = split(h2)
            for k, part in enumerate((h1h, h2h, h1l, h2l, h1h, h2h)):
                hs[2 * c + e, k * XY : (k + 1) * XY] = part
            h3s[2 * c + e] = h3

    def gauss(pair):
        for k, tile in zip(pair, at_gauss(jj, js, pair)):
            if partial is not None:
                tile = tile + partial[0][k]
            for d in range(3):
                start = (0, QQ, 4 * QQ)[d]
                gap = (2 * QQ, 2 * QQ, QQ)[d]
                high, low = split(u_ref[3 * d + k % 3] * tile)
                ts[k, start : start + QQ] = high
                ts[k, start + gap : start + gap + QQ] = low

    gauss(PAIRS[0])
    flux(0)
    gauss(PAIRS[1])
    flux(1)
    gauss(PAIRS[2])
    flux(2)
    gauss(PAIRS[3])
    gauss(PAIRS[4])


def back(part, tables, scratch, kept):
    z_back, back_12, back_3, div = tables
    ts, hs, h3s = kept
    bz = scratch["bz"]
    planes = PART_PLANES[part]
    count = 8 * len(planes)
    result = [[None, None] for _ in range(3)]
    sides = [{}, {}]
    for pair in PAIRS:
        for k, (table, depth, where) in enumerate(
            ((back_12, 4 * QQ, slice(0, 4 * QQ)), (back_3, 2 * QQ, slice(4 * QQ, None)))
        ):
            both = dot(wide(table, depth), tiles_at(ts, pair, where))
            both = both[:count] + both[count:]
            for tile, values in zip(pair, columns(both, len(pair))):
                sides[k][tile] = values
    for c in range(3):
        spread = columns(dot(wide(div), tiles_at(hs, (2 * c, 2 * c + 1))), 2)
        for e in range(2):
            result[c][e] = spread[e]
            rows = slice((2 * c + e) * count, (2 * c + e + 1) * count)
            for k in range(2):
                far = sides[k][3 * c + 2]
                far = far if e == 0 else pltpu.roll(far, 64, 1)
                for t, tile in enumerate((sides[k][3 * c + e], far)):
                    bz[4 * k + t, rows], bz[4 * k + t + 2, rows] = split(tile)
            bz[8, rows], bz[9, rows] = split(part_rows(part, h3s[2 * c + e]))
    out = fold(dot(wide(bz), wide(z_back)))
    for c in range(3):
        for e in range(2):
            result[c][e] += out[(2 * c + e) * count : (2 * c + e + 1) * count]
    return result


def part_rows(part, tall):
    return jnp.concatenate([tall[8 * x : 8 * x + 8] for x in PART_PLANES[part]], axis=0)


def sum_local(pair, out_ref, slot):
    shape = (out_ref.shape[1], 8, LANES)
    row = lax.broadcasted_iota(jnp.int32, shape, 1)
    lane = lax.broadcasted_iota(jnp.int32, shape, 2)
    inner = lane % 8
    for e in range(2):
        mine = pair[e].reshape(shape)
        other = pair[1 - e].reshape(shape)
        total = mine + jnp.where(row == 7, pltpu.roll(other, 7, 1), 0.0)
        total = total + jnp.where(row == 0, pltpu.roll(other, 1, 1), 0.0)
        after = pltpu.roll(total, LANES - 1, 2)
        before = pltpu.roll(total, 1, 2)
        total = (
            total
            + jnp.where((inner == 7) & (lane < LANES - 1), after, 0.0)
            + jnp.where((inner == 0) & (lane > 0), before, 0.0)
        )
        out_ref[slot, :, 8 * e : 8 * (e + 1), :] = total


def positions():
    c = lax.axis_index("col")
    return c % 2, c == 0, c == lax.axis_size("col") - 1


def places(ref):
    fields, planes = ref.shape[:2]
    return [
        (slot, x, e, (slot * planes + x) * 2 + e)
        for slot in range(fields)
        for x in range(planes)
        for e in range(2)
    ]


def pack_edges(sum_ref, edge_ref):
    lane = lax.broadcasted_iota(jnp.int32, (8, LANES), 1)
    packed = jnp.zeros((8, LANES), F32)
    for slot, x, e, at in places(sum_ref):
        tile = sum_ref[slot, x, 8 * e : 8 * (e + 1), :]
        packed = jnp.where(lane == 2 * at, pltpu.roll(tile, 2 * at, 1) if at else tile, packed)
        packed = jnp.where(lane == 2 * at + 1, pltpu.roll(tile, (2 * at + 2) % LANES, 1), packed)
    edge_ref[...] = packed


def with_edges(sum_ref, edge_refs):
    col_odd, _, _ = positions()
    lane = lax.broadcasted_iota(jnp.int32, (8, LANES), 1)
    edges = jnp.zeros((8, LANES), F32)
    for k, ref in enumerate(edge_refs):
        edges = edges + jnp.where(lane % 2 == (col_odd + k) % 2, ref[...], 0.0)
    meets = (lane == LANES - 1) | (lane == 0)
    return {
        (slot, x, e): sum_ref[slot, x, 8 * e : 8 * (e + 1), :]
        + jnp.where(meets, pltpu.roll(edges, LANES - 1 - 2 * at, 1), 0.0)
        for slot, x, e, at in places(sum_ref)
    }


def planes_kernel(count, *refs):
    outer, edge_refs, (up, down) = refs[0], refs[1 : 1 + count], refs[-2:]
    for (slot, x, e), tile in with_edges(outer, edge_refs).items():
        (up if x else down)[slot, 8 * e : 8 * (e + 1), :] = tile


def arrived(own_refs, up_ref, down_ref):
    up, down = own_refs
    return {
        (slot, x, e): (up if x else down)[slot, 8 * e : 8 * (e + 1), :]
        + (down_ref if x else up_ref)[slot, 8 * e : 8 * (e + 1), :]
        for slot, x, e, _ in places(jax.ShapeDtypeStruct((up.shape[0], 2, 16, LANES), F32))
    }


def interior_mask():
    _, first, last = positions()
    lane = lax.broadcasted_iota(jnp.int32, (1, LANES), 1)
    outer = ((lane == 0) & first) | ((lane == LANES - 1) & last)
    return jnp.where(outer, 0.0, 1.0)


def scale_metric(diag_ref, cross_ref, weights, metric):
    for k in range(6):
        ref = diag_ref if k < 3 else cross_ref
        block = ref[k % 3].astype(F32)
        for e in range(2):
            metric[k, e] = section_rows(block, e) * weights[...] * VISCOSITY


def finish(part, kept, tables, scratch, total, edge, mass=None):
    result = back(part, tables, scratch, kept)
    for c in range(3):
        sum_local(result[c], total, c)
    if mass is not None:
        jac, w = mass
        rows = [part_rows(part, section_rows(jac[...], e) * w[...]) for e in range(2)]
        sum_local(rows, total, 3)
    pack_edges(total, edge)


def back_tables(z_back, packed, ref, part):
    return [z_back] + [packed.get(ref, (kind, part)) for kind in ("back_12", "back_3", "div")]


def first_kernel(early_pack, rho, *refs):
    sources, refs = refs[:8], refs[8:]
    v, early, late, z_forward, z_back, jac, w, u, metric, *kept = refs[:12]
    total, edge, bases, b, gd, gc, sems = refs[12:19]
    bz, xhl, js, vs, flow_xhl, flow_js = refs[19:]
    targets = [bases, b, early, v, gd, gc, jac, late]
    copies = [
        pltpu.make_async_copy(source, target, sems.at[k])
        for k, (source, target) in enumerate(zip(sources, targets))
    ]
    for copy in copies:
        copy.start()
    copies[0].wait()
    build_wall_tables(bases, z_forward, z_back, w, rho)
    for copy in copies[1:7]:
        copy.wait()
    values, slopes = early_pack.get(early, "values"), early_pack.get(early, "slopes")
    wall_stage(lambda c, e: section_rows(b[c], e), z_forward, flow_xhl, flow_js)
    by_wall = wall_stage(lambda c, e: section_rows(v[c], e), z_forward, xhl, js, vs)
    fine_flow(values, flow_js, u)
    scale_metric(gd, gc, w, metric)
    front(by_wall, values, slopes, js, vs, u, metric, kept)
    tables = back_tables(z_back, early_pack, early, 0)
    finish(0, kept, tables, {"bz": bz}, total, edge, (jac, w))
    copies[7].wait()


def inner_kernel(has_mass, late_pack, *refs):
    kept, (z_back, late), refs = refs[:3], refs[3:5], refs[5:]
    mass, refs = (refs[:2], refs[2:]) if has_mass else (None, refs)
    total, edge, bz = refs
    tables = back_tables(z_back, late_pack, late, 1)
    finish(1, kept, tables, {"bz": bz}, total, edge, mass)


def half_step(part, tiles, v, inverse, half):
    mask = interior_mask()
    for k, x in enumerate(PART_PLANES[part]):
        for e in range(2):
            rows = slice(8 * e, 8 * (e + 1))
            inv = 1.0 / tiles[3, k, e]
            inverse[k, rows] = inv
            for c in range(3):
                step = (0.5 * STEP_SIZE) * inv * tiles[c, k, e]
                half[c, e, 8 * k : 8 * (k + 1)] = mask * (v[c, x, rows] - step)


def prepare_kernel(edges, late_pack, *refs):
    v, z_forward, late, summed = refs[:4]
    inverse, values, slopes, wall_slopes, half, xhl, js, vs = refs[4 + edges :]
    jj, grads = late_pack.get(late, ("values", 1)), late_pack.get(late, ("slopes", 1))
    half_step(1, with_edges(summed, refs[4 : 4 + edges]), v, inverse, half)
    by_wall = wall_stage(lambda c, e: half[c, e], z_forward, xhl, js, vs)
    for pair in PAIRS:
        for k, tile in zip(pair, at_gauss(jj, js, pair)):
            values[k] = tile
    for c in range(3):
        for e, both in enumerate(section_slopes(grads, vs, c)):
            slopes[2 * c + e] = both
            wall_slopes[2 * c + e] = by_wall[c, e]


def second_kernel(early_pack, late_pack, *refs):
    v, z_forward, z_back, early, late, u, metric = refs[:7]
    values, slopes, wall_slopes, up, down, up_in, down_in = refs[7:14]
    inverse, kept, (total, edge) = refs[14], refs[15:18], refs[18:20]
    bz, xhl, js, vs, half = refs[20:]
    jj, grads = late_pack.get(late, ("values", 0)), late_pack.get(late, ("slopes", 0))
    half_step(0, arrived((up, down), up_in, down_in), v, inverse, half)
    by_wall = wall_stage(lambda c, e: half[c, e], z_forward, xhl, js, vs)
    for (c, e), outer in by_wall.items():
        inner = wall_slopes[2 * c + e]
        by_wall[c, e] = jnp.concatenate([outer[:8], inner, outer[8:]], axis=0)
    front(by_wall, jj, grads, js, vs, u, metric, kept, (values, slopes))
    tables = back_tables(z_back, early_pack, early, 0)
    finish(0, kept, tables, {"bz": bz}, total, edge)


def advance(part, tiles, v, inverse, held):
    mask = interior_mask()
    planes = PART_PLANES[part]
    for c in range(3):
        for k, x in enumerate(planes):
            for e in range(2):
                rows = slice(8 * e, 8 * (e + 1))
                step = STEP_SIZE * inverse[k, rows] * tiles[c, k, e]
                held[c, k, rows] = mask * (v[c, x, rows] - step)


def advance_inner_kernel(edges, *refs):
    v, inverse, summed = refs[:3]
    advance(1, with_edges(summed, refs[3 : 3 + edges]), v, inverse, refs[-1])


def advance_kernel(*refs):
    v, inverse, inner, up, down, up_in, down_in, out, held, sems = refs
    copies = [pltpu.make_async_copy(inner, out.at[:, 1:7], sems.at[0])]
    copies[0].start()
    advance(0, arrived((up, down), up_in, down_in), v, inverse, held)
    for k, x in enumerate(PART_PLANES[0]):
        copies.append(pltpu.make_async_copy(held.at[:, k], out.at[:, x], sems.at[1 + k]))
        copies[-1].start()
    for copy in copies:
        copy.wait()


def back_scratch(part):
    return [pltpu.VMEM((10, 6 * 8 * len(PART_PLANES[part]), LANES), BF16)]


def front_scratch(count, with_field=True):
    shapes = [(2, 2, 3 * count, LANES), (9, 3 * count, LANES), (6, 3 * count, LANES)]
    return [pltpu.VMEM(shape, BF16) for shape in shapes[: 3 if with_field else 2]]


def call(kernel, name, ins, outs, scratch, in_space=pltpu.VMEM, out_space=pltpu.VMEM):
    ins = [pltpu.with_memory_space_constraint(array, in_space) for array in ins]
    return pl.pallas_call(
        kernel,
        name=name,
        out_shape=[out_space(shape, dtype) for shape, dtype in outs],
        in_specs=[pl.BlockSpec(memory_space=in_space)] * len(ins),
        out_specs=[pl.BlockSpec(memory_space=out_space)] * len(outs),
        scratch_shapes=scratch,
        compiler_params=pltpu.CompilerParams(vmem_limit_bytes=24 * 1024 * 1024),
    )(*ins)


def wall_pairings(count):
    even = [(i, i + 1) for i in range(0, count - 1, 2)]
    odd = [(i, i + 1) for i in range(1, count - 1, 2)]
    return [pairs + [(b, a) for a, b in pairs] for pairs in (even, odd) if pairs]


def swap_edges(edge):
    return [lax.ppermute(edge, "col", way) for way in wall_pairings(lax.axis_size("col"))]


def local(adjoint_field, base_flow, metric_diag, metric_cross, jacobian):
    early_pack, late_pack = Packed(EARLY), Packed(LATE)
    bases, rho = wall_bases()
    block = adjoint_field.shape[1:]
    field = ((3,) + block, F32)
    kept_shapes = [
        ((9, 6 * QQ, LANES), BF16),
        ((6, 6 * XY, LANES), BF16),
        ((6, XY, LANES), F32),
    ]
    edge_shape = ((8, LANES), F32)
    spans = lax.axis_size("span")
    ahead = [(i, (i + 1) % spans) for i in range(spans)]
    back_way = [(b, a) for a, b in ahead]

    def sums(fields, part):
        return [((fields, len(PART_PLANES[part])) + block[1:], F32), edge_shape]

    def exchange(fields, outer, outer_edge, operands):
        outer_edges = swap_edges(outer_edge)
        inner, inner_edge = call(
            functools.partial(inner_kernel, len(operands) > 5, late_pack),
            "inner_planes",
            operands,
            sums(fields, 1),
            back_scratch(1),
        )
        up, down = call(
            functools.partial(planes_kernel, len(outer_edges)),
            "planes",
            [outer] + outer_edges + [inner_edge],
            [((fields,) + block[1:], F32)] * 2,
            [],
        )
        inner_edges = swap_edges(inner_edge)
        up_in, down_in = lax.ppermute(up, "span", ahead), lax.ppermute(down, "span", back_way)
        return [up, down, up_in, down_in], inner, inner_edges

    early, late = (jnp.asarray(pack.array, BF16) for pack in (early_pack, late_pack))
    ins = [jnp.asarray(bases), base_flow, early, adjoint_field]
    ins += [metric_diag, metric_cross, jacobian, late]
    v, early, late, z_forward, z_back, jac, w, u, metric, *kept, outer, outer_edge = call(
        functools.partial(first_kernel, early_pack, rho),
        "first_operator",
        ins,
        [field, (early.shape, BF16), (late.shape, BF16)]
        + [((6, 2 * LANES, LANES), BF16), ((2, 1280, LANES), BF16)]
        + [(block, F32), ((XY, LANES), F32)]
        + [((9, QQ, LANES), F32), ((6, 2, XY, LANES), F32)]
        + kept_shapes
        + sums(4, 0),
        [
            pltpu.VMEM(bases.shape, F32),
            pltpu.VMEM((3,) + block, F32),
            pltpu.VMEM((3,) + block, BF16),
            pltpu.VMEM((3,) + block, BF16),
            pltpu.SemaphoreType.DMA((len(ins),)),
        ]
        + back_scratch(0)
        + front_scratch(XY)
        + front_scratch(XY, False),
        in_space=pltpu.HBM,
    )
    planes, inner, inner_edges = exchange(4, outer, outer_edge, kept + [z_back, late, jac, w])
    half = [pltpu.VMEM((3, 2, 8 * len(planes), LANES), F32) for planes in PART_PLANES]
    inner_inverse, *partial = call(
        functools.partial(prepare_kernel, len(inner_edges), late_pack),
        "prepare",
        [v, z_forward, late, inner] + inner_edges,
        [
            ((6,) + block[1:], F32),
            ((9, QQ, LANES), F32),
            ((6, 2 * XY, LANES), F32),
            ((6, 48, LANES), F32),
        ],
        [half[1]] + front_scratch(48),
    )
    inverse, *kept, outer, outer_edge = call(
        functools.partial(second_kernel, early_pack, late_pack),
        "second_operator",
        [v, z_forward, z_back, early, late, u, metric] + partial + planes,
        [((2,) + block[1:], F32)] + kept_shapes + sums(3, 0),
        back_scratch(0) + front_scratch(16) + [half[0]],
    )
    planes, inner, inner_edges = exchange(3, outer, outer_edge, kept + [z_back, late])
    (done,) = call(
        functools.partial(advance_inner_kernel, len(inner_edges)),
        "advance_inner",
        [v, inner_inverse, inner] + inner_edges,
        [((3, 6) + block[1:], F32)],
        [],
    )
    (out,) = call(
        advance_kernel,
        "advance",
        [v, inverse, done] + planes,
        [field],
        [pltpu.VMEM((3, 2) + block[1:], F32), pltpu.SemaphoreType.DMA((3,))],
        out_space=pltpu.HBM,
    )
    return out


def solution(mesh):
    in_specs = (
        P(None, "span", None, "col"),
        P(None, "span", None, "col"),
        P(None, "span", None, "col"),
        P(None, "span", None, "col"),
        P("span", None, "col"),
    )
    out_specs = P(None, "span", None, "col")
    return jax.shard_map(local, mesh=mesh, in_specs=in_specs, out_specs=out_specs, check_vma=False)
```

```python
import functools

import jax
import jax.numpy as jnp
import numpy as np
from jax import lax
from jax.experimental import pallas as pl
from jax.experimental.pallas import tpu as pltpu
from jax.sharding import PartitionSpec as P

VISCOSITY = 0.05
STEP_SIZE = 0.01
GLL_INNER = [
    -0.8717401485096066,
    -0.5917001814331423,
    -0.2092992179024789,
    0.2092992179024789,
    0.5917001814331423,
    0.8717401485096066,
]
GAUSS_POINTS = [
    -0.9815606342467192,
    -0.9041172563704749,
    -0.7699026741943047,
    -0.5873179542866175,
    -0.3678314989981802,
    -0.1252334085114689,
    0.1252334085114689,
    0.3678314989981802,
    0.5873179542866175,
    0.7699026741943047,
    0.9041172563704749,
    0.9815606342467192,
]
GAUSS_WEIGHTS = [
    0.0471753363865118,
    0.1069393259953184,
    0.1600783285433462,
    0.2031674267230659,
    0.2334925365383548,
    0.2491470458134028,
    0.2491470458134028,
    0.2334925365383548,
    0.2031674267230659,
    0.1600783285433462,
    0.1069393259953184,
    0.0471753363865118,
]
F32 = jnp.float32
BF16 = jnp.bfloat16
XY = 64
QQ = 144
LANES = 128
PART_PLANES = ([0, 7], [1, 2, 3, 4, 5, 6])
PART_ROWS = [[8 * x + y for x in planes for y in range(8)] for planes in PART_PLANES]
ROWS = PART_ROWS[0] + PART_ROWS[1]
PAIRS = [(0, 1), (2, 3), (4, 5), (6, 7), (8,)]


def legendre_seven(points):
    previous = points * 0.0 + 1.0
    current = points
    for degree in range(1, 7):
        following = ((2.0 * degree + 1.0) * points * current - degree * previous) / (degree + 1.0)
        previous = current
        current = following
    return current


def node_tables():
    gll_nodes = np.array([-1.0] + GLL_INNER + [1.0])
    values = legendre_seven(gll_nodes)
    node_weights = 2.0 / (56.0 * values * values)
    identity = np.eye(8, dtype=bool)
    spacing = gll_nodes[:, None] - gll_nodes[None, :]
    derivative = np.where(
        identity, 0.0, values[:, None] / (values[None, :] * np.where(identity, 1.0, spacing))
    )
    corner_terms = np.concatenate([np.array([-14.0]), np.zeros(6), np.array([14.0])])
    derivative = derivative + np.eye(8) * corner_terms[None, :]
    gauss_nodes = np.array(GAUSS_POINTS)
    gauss_weights = np.array(GAUSS_WEIGHTS)
    numerators = gauss_nodes[:, None, None] - gll_nodes[None, None, :]
    denominators = np.where(identity, 1.0, spacing)[None]
    ratios = np.where(identity[None], 1.0, numerators / denominators)
    interpolation = ratios.prod(axis=2)
    slope_interp = interpolation @ derivative
    return (derivative, node_weights, interpolation, slope_interp, gauss_weights)


def halves(matrix):
    high = np.asarray(matrix, np.float32).astype(jnp.bfloat16)
    low = (np.asarray(matrix, np.float64) - high.astype(np.float64)).astype(jnp.bfloat16)
    return high, low


def lane_tiles(table):
    rows, columns = table.shape
    padded = np.pad(table, ((0, 0), (0, -columns % LANES)))
    return padded.reshape(rows, -1, LANES).transpose(1, 0, 2)


def part_rows(part, tall):
    return tall[16:] if part else tall[:16]


def three(matrix):
    high, low = halves(matrix)
    return np.concatenate([high, high, low], axis=1)


def stacked(matrix):
    high, low = halves(matrix)
    upper = np.concatenate([high, high], axis=1)
    return np.concatenate([upper, np.concatenate([low, np.zeros_like(low)], axis=1)], axis=0)


def section_tables():
    dm, _, jm, dj, sigma = node_tables()
    eye = np.eye(8)
    values = np.kron(jm, jm)[:, ROWS]
    along = [np.kron(dm, eye)[ROWS][:, ROWS], np.kron(eye, dm)[ROWS][:, ROWS]]
    slopes = np.concatenate(along, axis=0)
    js, ds = sigma[:, None] * jm, sigma[:, None] * dj
    back_12 = np.concatenate([np.kron(ds, js).T, np.kron(js, ds).T], axis=1)
    back_3 = np.kron(js, js).T
    div = np.concatenate([matrix.T for matrix in along], axis=1)
    tables = {"values": three(values), "slopes": three(slopes)}
    for part, rows in enumerate(PART_ROWS):
        tables["back_12", part] = stacked(back_12[rows])
        tables["back_3", part] = stacked(back_3[rows])
        tables["div", part] = three(part_rows(part, div))
    return {name: lane_tiles(table) for name, table in tables.items()}


EARLY = ["values", "slopes", ("back_12", 0), ("back_3", 0), ("div", 0)]
LATE = [("back_12", 1), ("back_3", 1), ("div", 1)]


class Packed:
    def __init__(self, names):
        tables = section_tables()
        self.array = np.concatenate([tables[name].reshape(-1, LANES) for name in names])
        self.places, start = {}, 0
        for name in names:
            self.places[name] = (start, tables[name].shape)
            start += tables[name].shape[0] * tables[name].shape[1]

    def get(self, ref, name):
        start, (tiles, rows, _) = self.places[name]
        return [ref[start + k * rows : start + (k + 1) * rows] for k in range(tiles)]


def wall_bases():
    dm, rho, jm, dj, sigma = node_tables()
    lane = np.arange(LANES)
    gauss = np.arange(24)
    forward_lanes = [lane % 12, (lane + LANES) % 12]
    blocks = [dm.T[:, lane % 8]]
    blocks += [jm.T[:, lanes] for lanes in forward_lanes]
    blocks[2] = np.where(lane < 64, blocks[2], 0.0)
    blocks += [(sigma[:, None] * matrix)[gauss % 12][:, lane % 8] for matrix in (jm, dj)]
    blocks += [dm[:, lane % 8]]
    rows = [np.asarray(part, np.float32) for block in blocks for part in halves(block)]
    rows.append(np.asarray(rho[:, None] * rho[None, lane % 8], np.float32))
    return np.concatenate(rows), [float(weight) for weight in rho]


def build_wall_tables(bases, z_forward, z_back, w, rho):
    row = lax.broadcasted_iota(jnp.int32, (8, LANES), 0)
    lane = lax.broadcasted_iota(jnp.int32, (8, LANES), 1)
    zero = jnp.zeros((8, LANES), F32)
    nothing = jnp.zeros((LANES, LANES), BF16)
    for t in range(6):
        kind, low = t // 2, t % 2
        element = (lane // 8, lane // 12, (lane + LANES) // 12)[kind]
        base = bases[8 * t : 8 * t + 8]
        table = [jnp.where(element == a, base, zero) for a in range(16)]
        table = jnp.concatenate(table, axis=0).astype(BF16)
        z_forward[t, :LANES] = table
        z_forward[t, LANES:] = nothing if low else table
    for kind in range(2):
        for low in range(2):
            start = 48 + 24 * (2 * kind + low)
            table = []
            for block in range(24):
                inside = row + 8 * block - 12 * (lane // 8)
                base = bases[start + 8 * (block % 3) : start + 8 * (block % 3) + 8]
                table.append(jnp.where((inside >= 0) & (inside < 12), base, zero))
            table = jnp.concatenate(table + [zero] * 8, axis=0).astype(BF16)
            z_back[low, 512 * kind : 512 * kind + 256] = table
            z_back[low, 512 * kind + 256 : 512 * (kind + 1)] = (
                jnp.zeros((256, LANES), BF16) if low else table
            )
    for low in range(2):
        base = bases[144 + 8 * low : 152 + 8 * low]
        table = [jnp.where(lane // 8 == a, base, zero) for a in range(16)]
        table = jnp.concatenate(table, axis=0).astype(BF16)
        z_back[low, 1024:1152] = table
        z_back[low, 1152:] = nothing if low else table
    for x in range(8):
        w[8 * x : 8 * x + 8] = bases[160:168] * rho[ROWS[8 * x] // 8]


def split(values):
    high = values.astype(BF16)
    low = (values - high.astype(F32)).astype(BF16)
    return high, low


def dot(left, right):
    return jnp.dot(left, right, preferred_element_type=F32)


def wide(tiles, columns=None):
    count = len(tiles) if isinstance(tiles, list) else tiles.shape[0]
    whole = jnp.concatenate([tiles[k] for k in range(count)], axis=1)
    return whole if columns is None else whole[:, :columns]


def fold(values):
    return values[:, :LANES] + values[:, LANES : 2 * LANES]


def section_rows(block, e):
    planes = block.reshape(8, 2, 8, LANES)[:, e]
    planes = jnp.concatenate([planes[:1], planes[7:], planes[1:7]], axis=0)
    return planes.reshape(XY, LANES)


def tiles_at(ref, tiles, rows=slice(None)):
    return jnp.concatenate([ref[k, rows] for k in tiles], axis=1)


def columns(values, count):
    return [values[:, k * LANES : (k + 1) * LANES] for k in range(count)]


def wall_stage(rows_of, z_forward, xhl, js, vs=None):
    count = js.shape[1] // 3
    skip = 2 if vs is None else 0
    batches = [[(c, e) for c in range(3)] for e in range(2)]
    if count < 32:
        batches = [batches[0] + batches[1]]
    pieces = {}
    for first, batch in enumerate(batches):
        start = first * 3 * count
        for k, (c, e) in enumerate(batch):
            rows = slice(start + k * count, start + (k + 1) * count)
            high, low = split(rows_of(c, e))
            xhl[0, rows], xhl[1, rows] = high, low
            if vs is not None:
                for t, part in enumerate((high, low, high)):
                    vs[2 * c + e, t * count : (t + 1) * count] = part
        out = dot(wide(xhl.at[:, start : start + len(batch) * count]), wide(z_forward.at[skip:]))
        for k, (c, e) in enumerate(batch):
            for kind in range(skip // 2, 3):
                lanes = slice((2 * kind - skip) * LANES, (2 * kind - skip + 2) * LANES)
                pieces[kind, c, e] = fold(out[k * count : (k + 1) * count, lanes])
    for c in range(3):
        tiles = [pieces[1, c, 0], pieces[1, c, 1]]
        tiles.append(pieces[2, c, 0] + pltpu.roll(pieces[2, c, 1], 64, 1))
        for t, tile in enumerate(tiles):
            high, low = split(tile)
            for k, part in enumerate((high, low, high)):
                js[3 * c + t, k * count : (k + 1) * count] = part
    return {(c, e): pieces[0, c, e] for c in range(3) for e in range(2)} if vs is not None else None


def right_side(refs, tiles):
    whole = []
    for k in tiles:
        parts = []
        for third in range(3):
            for ref in refs:
                count = ref.shape[1] // 3
                parts.append(ref[k, third * count : (third + 1) * count])
        whole.append(jnp.concatenate(parts, axis=0))
    return jnp.concatenate(whole, axis=1)


def at_gauss(jj, js, pair):
    return columns(dot(wide(jj, 3 * XY), right_side(js, pair)), len(pair))


def section_slopes(grads, vs, c):
    return columns(dot(wide(grads, 3 * XY), right_side(vs, (2 * c, 2 * c + 1))), 2)


def fine_flow(jj, js, u_ref):
    for pair in PAIRS:
        for k, tile in zip(pair, at_gauss(jj, js, pair)):
            u_ref[k] = tile


def front(slopes, jj, grads, js, vs, u_ref, metric, kept):
    ts, hs, h3s = kept

    def flux(c):
        for e, both in enumerate(section_slopes(grads, vs, c)):
            g1, g2, g3 = both[:XY], both[XY:], slopes[c, e]
            m11, m22, m33, m12, m13, m23 = (metric[k, e] for k in range(6))
            h1 = m11 * g1 + m12 * g2 + m13 * g3
            h2 = m12 * g1 + m22 * g2 + m23 * g3
            h3 = m13 * g1 + m23 * g2 + m33 * g3
            h1h, h1l = split(h1)
            h2h, h2l = split(h2)
            for k, part in enumerate((h1h, h2h, h1l, h2l, h1h, h2h)):
                hs[2 * c + e, k * XY : (k + 1) * XY] = part
            h3s[2 * c + e] = h3

    def gauss(pair):
        for k, tile in zip(pair, at_gauss(jj, js, pair)):
            for d in range(3):
                start = (0, QQ, 4 * QQ)[d]
                gap = (2 * QQ, 2 * QQ, QQ)[d]
                high, low = split(u_ref[3 * d + k % 3] * tile)
                ts[k, start : start + QQ] = high
                ts[k, start + gap : start + gap + QQ] = low

    if len(js) == 1:
        work = [(gauss, pair) for pair in PAIRS] + [(flux, c) for c in range(3)]
    else:
        work = [step for c in range(3) for step in ((flux, c), (gauss, PAIRS[c]))]
        work += [(gauss, pair) for pair in PAIRS[3:]]
    for step, argument in work:
        step(argument)


def back(part, tables, scratch, kept):
    z_back, back_12, back_3, div = tables
    ts, hs, h3s = kept
    bz = scratch["bz"]
    planes = PART_PLANES[part]
    count = 8 * len(planes)
    result = [[None, None] for _ in range(3)]
    sides = [{}, {}]
    for pair in PAIRS:
        for k, (table, depth, where) in enumerate(
            ((back_12, 4 * QQ, slice(0, 4 * QQ)), (back_3, 2 * QQ, slice(4 * QQ, None)))
        ):
            both = dot(wide(table, depth), tiles_at(ts, pair, where))
            both = both[:count] + both[count:]
            for tile, values in zip(pair, columns(both, len(pair))):
                sides[k][tile] = values
    for c in range(3):
        spread = columns(dot(wide(div), tiles_at(hs, (2 * c, 2 * c + 1))), 2)
        for e in range(2):
            result[c][e] = spread[e]
            rows = slice((2 * c + e) * count, (2 * c + e + 1) * count)
            for k in range(2):
                far = sides[k][3 * c + 2]
                far = far if e == 0 else pltpu.roll(far, 64, 1)
                for t, tile in enumerate((sides[k][3 * c + e], far)):
                    bz[4 * k + t, rows], bz[4 * k + t + 2, rows] = split(tile)
            bz[8, rows], bz[9, rows] = split(part_rows(part, h3s[2 * c + e]))
    out = fold(dot(wide(bz), wide(z_back)))
    for c in range(3):
        for e in range(2):
            result[c][e] += out[(2 * c + e) * count : (2 * c + e + 1) * count]
    return result


def sum_local(pair, out_ref, slot):
    shape = (out_ref.shape[1], 8, LANES)
    row = lax.broadcasted_iota(jnp.int32, shape, 1)
    lane = lax.broadcasted_iota(jnp.int32, shape, 2)
    inner = lane % 8
    for e in range(2):
        mine = pair[e].reshape(shape)
        other = pair[1 - e].reshape(shape)
        total = mine + jnp.where(row == 7, pltpu.roll(other, 7, 1), 0.0)
        total = total + jnp.where(row == 0, pltpu.roll(other, 1, 1), 0.0)
        after = pltpu.roll(total, LANES - 1, 2)
        before = pltpu.roll(total, 1, 2)
        total = (
            total
            + jnp.where((inner == 7) & (lane < LANES - 1), after, 0.0)
            + jnp.where((inner == 0) & (lane > 0), before, 0.0)
        )
        out_ref[slot, :, 8 * e : 8 * (e + 1), :] = total


def positions():
    c = lax.axis_index("col")
    return c % 2, c == 0, c == lax.axis_size("col") - 1


def places(ref):
    fields, planes = ref.shape[:2]
    return [
        (slot, x, e, (slot * planes + x) * 2 + e)
        for slot in range(fields)
        for x in range(planes)
        for e in range(2)
    ]


def pack_edges(sum_ref, edge_ref):
    lane = lax.broadcasted_iota(jnp.int32, (8, LANES), 1)
    packed = jnp.zeros((8, LANES), F32)
    for slot, x, e, at in places(sum_ref):
        tile = sum_ref[slot, x, 8 * e : 8 * (e + 1), :]
        packed = jnp.where(lane == 2 * at, pltpu.roll(tile, 2 * at, 1) if at else tile, packed)
        packed = jnp.where(lane == 2 * at + 1, pltpu.roll(tile, (2 * at + 2) % LANES, 1), packed)
    edge_ref[...] = packed


def with_edges(sum_ref, edge_refs):
    col_odd, _, _ = positions()
    lane = lax.broadcasted_iota(jnp.int32, (8, LANES), 1)
    edges = jnp.zeros((8, LANES), F32)
    for k, ref in enumerate(edge_refs):
        edges = edges + jnp.where(lane % 2 == (col_odd + k) % 2, ref[...], 0.0)
    meets = (lane == LANES - 1) | (lane == 0)
    return {
        (slot, x, e): sum_ref[slot, x, 8 * e : 8 * (e + 1), :]
        + jnp.where(meets, pltpu.roll(edges, LANES - 1 - 2 * at, 1), 0.0)
        for slot, x, e, at in places(sum_ref)
    }


def planes_kernel(count, *refs):
    outer, edge_refs, (up, down) = refs[0], refs[1 : 1 + count], refs[-2:]
    for (slot, x, e), tile in with_edges(outer, edge_refs).items():
        (up if x else down)[slot, 8 * e : 8 * (e + 1), :] = tile


def arrived(own_refs, up_ref, down_ref):
    up, down = own_refs
    return {
        (slot, x, e): (up if x else down)[slot, 8 * e : 8 * (e + 1), :]
        + (down_ref if x else up_ref)[slot, 8 * e : 8 * (e + 1), :]
        for slot, x, e, _ in places(jax.ShapeDtypeStruct((up.shape[0], 2, 16, LANES), F32))
    }


def interior_mask():
    _, first, last = positions()
    lane = lax.broadcasted_iota(jnp.int32, (1, LANES), 1)
    outer = ((lane == 0) & first) | ((lane == LANES - 1) & last)
    return jnp.where(outer, 0.0, 1.0)


def scale_metric(diag_ref, cross_ref, weights, metric):
    for k in range(6):
        ref = diag_ref if k < 3 else cross_ref
        block = ref[k % 3].astype(F32)
        for e in range(2):
            metric[k, e] = section_rows(block, e) * weights[...] * VISCOSITY


def finish(part, kept, tables, scratch, total, edge, mass=None):
    result = back(part, tables, scratch, kept)
    for c in range(3):
        sum_local(result[c], total, c)
    if mass is not None:
        jac, w = mass
        rows = [part_rows(part, section_rows(jac[...], e) * w[...]) for e in range(2)]
        sum_local(rows, total, 3)
    pack_edges(total, edge)


def back_tables(z_back, packed, ref, part):
    return [z_back] + [packed.get(ref, (kind, part)) for kind in ("back_12", "back_3", "div")]


def first_kernel(early_pack, rho, *refs):
    sources, refs = refs[:8], refs[8:]
    v, early, late, z_forward, z_back, jac, w, u, metric, *kept = refs[:12]
    total, edge, bases, b, gd, gc, sems = refs[12:19]
    bz, xhl, js, vs, flow_xhl, flow_js = refs[19:]
    targets = [bases, b, v, early, gd, gc, jac, late]
    copies = [
        pltpu.make_async_copy(source, target, sems.at[k])
        for k, (source, target) in enumerate(zip(sources, targets))
    ]
    for copy in copies:
        copy.start()
    copies[0].wait()
    build_wall_tables(bases, z_forward, z_back, w, rho)
    copies[1].wait()
    copies[2].wait()
    wall_stage(lambda c, e: section_rows(b[c], e), z_forward, flow_xhl, flow_js)
    by_wall = wall_stage(lambda c, e: section_rows(v[c], e), z_forward, xhl, js, vs)
    copies[3].wait()
    copies[4].wait()
    copies[5].wait()
    copies[6].wait()
    values, slopes = early_pack.get(early, "values"), early_pack.get(early, "slopes")
    fine_flow(values, [flow_js], u)
    scale_metric(gd, gc, w, metric)
    front(by_wall, values, slopes, [js], [vs], u, metric, kept)
    tables = back_tables(z_back, early_pack, early, 0)
    finish(0, kept, tables, {"bz": bz}, total, edge, (jac, w))
    copies[7].wait()


def inner_kernel(has_mass, late_pack, *refs):
    kept, (z_back, late), refs = refs[:3], refs[3:5], refs[5:]
    mass, refs = (refs[:2], refs[2:]) if has_mass else (None, refs)
    total, edge, bz = refs
    tables = back_tables(z_back, late_pack, late, 1)
    finish(1, kept, tables, {"bz": bz}, total, edge, mass)


def half_step(part, tiles, v, inverse, half):
    mask = interior_mask()
    for k, x in enumerate(PART_PLANES[part]):
        for e in range(2):
            rows = slice(8 * e, 8 * (e + 1))
            inv = 1.0 / tiles[3, k, e]
            inverse[k, rows] = inv
            for c in range(3):
                step = (0.5 * STEP_SIZE) * inv * tiles[c, k, e]
                half[c, e, 8 * k : 8 * (k + 1)] = mask * (v[c, x, rows] - step)


def prepare_kernel(edges, *refs):
    v, z_forward, summed = refs[:3]
    inverse, js, vs, wall_slopes, half, xhl = refs[3 + edges :]
    half_step(1, with_edges(summed, refs[3 : 3 + edges]), v, inverse, half)
    by_wall = wall_stage(lambda c, e: half[c, e], z_forward, xhl, js, vs)
    for (c, e), slope in by_wall.items():
        wall_slopes[2 * c + e] = slope


def second_kernel(early_pack, *refs):
    v, z_forward, z_back, early, u, metric = refs[:6]
    inner_js, inner_vs, wall_slopes, up, down, up_in, down_in = refs[6:13]
    inverse, kept, (total, edge) = refs[13], refs[14:17], refs[17:19]
    bz, xhl, js, vs, half = refs[19:]
    values, slopes = early_pack.get(early, "values"), early_pack.get(early, "slopes")
    half_step(0, arrived((up, down), up_in, down_in), v, inverse, half)
    by_wall = wall_stage(lambda c, e: half[c, e], z_forward, xhl, js, vs)
    for c, e in by_wall:
        by_wall[c, e] = jnp.concatenate([by_wall[c, e], wall_slopes[2 * c + e]], axis=0)
    front(by_wall, values, slopes, [js, inner_js], [vs, inner_vs], u, metric, kept)
    tables = back_tables(z_back, early_pack, early, 0)
    finish(0, kept, tables, {"bz": bz}, total, edge)


def advance(part, tiles, v, inverse, held):
    mask = interior_mask()
    planes = PART_PLANES[part]
    for c in range(3):
        for k, x in enumerate(planes):
            for e in range(2):
                rows = slice(8 * e, 8 * (e + 1))
                step = STEP_SIZE * inverse[k, rows] * tiles[c, k, e]
                held[c, k, rows] = mask * (v[c, x, rows] - step)


def advance_inner_kernel(edges, *refs):
    v, inverse, summed = refs[:3]
    advance(1, with_edges(summed, refs[3 : 3 + edges]), v, inverse, refs[-1])


def advance_kernel(*refs):
    v, inverse, inner, up, down, up_in, down_in, out, held, sems = refs
    copies = [pltpu.make_async_copy(inner, out.at[:, 1:7], sems.at[0])]
    copies[0].start()
    advance(0, arrived((up, down), up_in, down_in), v, inverse, held)
    for k, x in enumerate(PART_PLANES[0]):
        copies.append(pltpu.make_async_copy(held.at[:, k], out.at[:, x], sems.at[1 + k]))
        copies[-1].start()
    for copy in copies:
        copy.wait()


def back_scratch(part):
    return [pltpu.VMEM((10, 6 * 8 * len(PART_PLANES[part]), LANES), BF16)]


def front_scratch(count, with_field=True):
    shapes = [(2, 6 * count, LANES), (9, 3 * count, LANES), (6, 3 * count, LANES)]
    return [pltpu.VMEM(shape, BF16) for shape in shapes[: 3 if with_field else 2]]


def call(kernel, name, ins, outs, scratch, in_space=pltpu.VMEM, out_space=pltpu.VMEM):
    ins = [pltpu.with_memory_space_constraint(array, in_space) for array in ins]
    return pl.pallas_call(
        kernel,
        name=name,
        out_shape=[out_space(shape, dtype) for shape, dtype in outs],
        in_specs=[pl.BlockSpec(memory_space=in_space)] * len(ins),
        out_specs=[pl.BlockSpec(memory_space=out_space)] * len(outs),
        scratch_shapes=scratch,
        compiler_params=pltpu.CompilerParams(vmem_limit_bytes=24 * 1024 * 1024),
    )(*ins)


def wall_pairings(count):
    even = [(i, i + 1) for i in range(0, count - 1, 2)]
    odd = [(i, i + 1) for i in range(1, count - 1, 2)]
    return [pairs + [(b, a) for a, b in pairs] for pairs in (even, odd) if pairs]


def swap_edges(edge):
    return [lax.ppermute(edge, "col", way) for way in wall_pairings(lax.axis_size("col"))]


def local(adjoint_field, base_flow, metric_diag, metric_cross, jacobian):
    early_pack, late_pack = Packed(EARLY), Packed(LATE)
    bases, rho = wall_bases()
    block = adjoint_field.shape[1:]
    field = ((3,) + block, F32)
    kept_shapes = [
        ((9, 6 * QQ, LANES), BF16),
        ((6, 6 * XY, LANES), BF16),
        ((6, XY, LANES), F32),
    ]
    edge_shape = ((8, LANES), F32)
    spans = lax.axis_size("span")
    ahead = [(i, (i + 1) % spans) for i in range(spans)]
    back_way = [(b, a) for a, b in ahead]

    def sums(fields, part):
        return [((fields, len(PART_PLANES[part])) + block[1:], F32), edge_shape]

    def exchange(fields, outer, outer_edge, operands):
        outer_edges = swap_edges(outer_edge)
        inner, inner_edge = call(
            functools.partial(inner_kernel, len(operands) > 5, late_pack),
            "inner_planes",
            operands,
            sums(fields, 1),
            back_scratch(1),
        )
        up, down = call(
            functools.partial(planes_kernel, len(outer_edges)),
            "planes",
            [outer] + outer_edges + [inner_edge],
            [((fields,) + block[1:], F32)] * 2,
            [],
        )
        inner_edges = swap_edges(inner_edge)
        up_in, down_in = lax.ppermute(up, "span", ahead), lax.ppermute(down, "span", back_way)
        return [up, down, up_in, down_in], inner, inner_edges

    early, late = (jnp.asarray(pack.array, BF16) for pack in (early_pack, late_pack))
    ins = [jnp.asarray(bases), base_flow, adjoint_field, early]
    ins += [metric_diag, metric_cross, jacobian, late]
    v, early, late, z_forward, z_back, jac, w, u, metric, *kept, outer, outer_edge = call(
        functools.partial(first_kernel, early_pack, rho),
        "first_operator",
        ins,
        [field, (early.shape, BF16), (late.shape, BF16)]
        + [((6, 2 * LANES, LANES), BF16), ((2, 1280, LANES), BF16)]
        + [(block, F32), ((XY, LANES), F32)]
        + [((9, QQ, LANES), F32), ((6, 2, XY, LANES), F32)]
        + kept_shapes
        + sums(4, 0),
        [
            pltpu.VMEM(bases.shape, F32),
            pltpu.VMEM((3,) + block, F32),
            pltpu.VMEM((3,) + block, BF16),
            pltpu.VMEM((3,) + block, BF16),
            pltpu.SemaphoreType.DMA((len(ins),)),
        ]
        + back_scratch(0)
        + front_scratch(XY)
        + front_scratch(XY, False),
        in_space=pltpu.HBM,
    )
    planes, inner, inner_edges = exchange(4, outer, outer_edge, kept + [z_back, late, jac, w])
    half = [pltpu.VMEM((3, 2, 8 * len(planes), LANES), F32) for planes in PART_PLANES]
    inner_inverse, *prepared = call(
        functools.partial(prepare_kernel, len(inner_edges)),
        "prepare",
        [v, z_forward, inner] + inner_edges,
        [
            ((6,) + block[1:], F32),
            ((9, 144, LANES), BF16),
            ((6, 144, LANES), BF16),
            ((6, 48, LANES), F32),
        ],
        [half[1], front_scratch(48)[0]],
    )
    inverse, *kept, outer, outer_edge = call(
        functools.partial(second_kernel, early_pack),
        "second_operator",
        [v, z_forward, z_back, early, u, metric] + prepared + planes,
        [((2,) + block[1:], F32)] + kept_shapes + sums(3, 0),
        back_scratch(0) + front_scratch(16) + [half[0]],
    )
    planes, inner, inner_edges = exchange(3, outer, outer_edge, kept + [z_back, late])
    (done,) = call(
        functools.partial(advance_inner_kernel, len(inner_edges)),
        "advance_inner",
        [v, inner_inverse, inner] + inner_edges,
        [((3, 6) + block[1:], F32)],
        [],
    )
    (out,) = call(
        advance_kernel,
        "advance",
        [v, inverse, done] + planes,
        [field],
        [pltpu.VMEM((3, 2) + block[1:], F32), pltpu.SemaphoreType.DMA((3,))],
        out_space=pltpu.HBM,
    )
    return out


def solution(mesh):
    in_specs = (
        P(None, "span", None, "col"),
        P(None, "span", None, "col"),
        P(None, "span", None, "col"),
        P(None, "span", None, "col"),
        P("span", None, "col"),
    )
    out_specs = P(None, "span", None, "col")
    return jax.shard_map(local, mesh=mesh, in_specs=in_specs, out_specs=out_specs, check_vma=False)
```

```python
import functools

import jax
import jax.numpy as jnp
import numpy as np
from jax import lax
from jax.experimental import pallas as pl
from jax.experimental.pallas import tpu as pltpu
from jax.sharding import PartitionSpec as P

VISCOSITY = 0.05
STEP_SIZE = 0.01
GLL_INNER = [
    -0.8717401485096066,
    -0.5917001814331423,
    -0.2092992179024789,
    0.2092992179024789,
    0.5917001814331423,
    0.8717401485096066,
]
GAUSS_POINTS = [
    -0.9815606342467192,
    -0.9041172563704749,
    -0.7699026741943047,
    -0.5873179542866175,
    -0.3678314989981802,
    -0.1252334085114689,
    0.1252334085114689,
    0.3678314989981802,
    0.5873179542866175,
    0.7699026741943047,
    0.9041172563704749,
    0.9815606342467192,
]
GAUSS_WEIGHTS = [
    0.0471753363865118,
    0.1069393259953184,
    0.1600783285433462,
    0.2031674267230659,
    0.2334925365383548,
    0.2491470458134028,
    0.2491470458134028,
    0.2334925365383548,
    0.2031674267230659,
    0.1600783285433462,
    0.1069393259953184,
    0.0471753363865118,
]
F32 = jnp.float32
BF16 = jnp.bfloat16
XY = 64
QQ = 144
LANES = 128
PART_PLANES = ([0, 7], [1, 2, 3, 4, 5, 6])
PART_ROWS = [[8 * x + y for x in planes for y in range(8)] for planes in PART_PLANES]
ROWS = PART_ROWS[0] + PART_ROWS[1]
PAIRS = [(0, 1), (2, 3), (4, 5), (6, 7), (8,)]


def legendre_seven(points):
    previous = points * 0.0 + 1.0
    current = points
    for degree in range(1, 7):
        following = ((2.0 * degree + 1.0) * points * current - degree * previous) / (degree + 1.0)
        previous = current
        current = following
    return current


def node_tables():
    gll_nodes = np.array([-1.0] + GLL_INNER + [1.0])
    values = legendre_seven(gll_nodes)
    node_weights = 2.0 / (56.0 * values * values)
    identity = np.eye(8, dtype=bool)
    spacing = gll_nodes[:, None] - gll_nodes[None, :]
    derivative = np.where(
        identity, 0.0, values[:, None] / (values[None, :] * np.where(identity, 1.0, spacing))
    )
    corner_terms = np.concatenate([np.array([-14.0]), np.zeros(6), np.array([14.0])])
    derivative = derivative + np.eye(8) * corner_terms[None, :]
    gauss_nodes = np.array(GAUSS_POINTS)
    gauss_weights = np.array(GAUSS_WEIGHTS)
    numerators = gauss_nodes[:, None, None] - gll_nodes[None, None, :]
    denominators = np.where(identity, 1.0, spacing)[None]
    ratios = np.where(identity[None], 1.0, numerators / denominators)
    interpolation = ratios.prod(axis=2)
    slope_interp = interpolation @ derivative
    return (derivative, node_weights, interpolation, slope_interp, gauss_weights)


def halves(matrix):
    high = np.asarray(matrix, np.float32).astype(jnp.bfloat16)
    low = (np.asarray(matrix, np.float64) - high.astype(np.float64)).astype(jnp.bfloat16)
    return high, low


def lane_tiles(table):
    rows, columns = table.shape
    padded = np.pad(table, ((0, 0), (0, -columns % LANES)))
    return padded.reshape(rows, -1, LANES).transpose(1, 0, 2)


def part_rows(part, tall):
    return tall[16:] if part else tall[:16]


def three(matrix):
    high, low = halves(matrix)
    return np.concatenate([high, high, low], axis=1)


def stacked(matrix):
    high, low = halves(matrix)
    upper = np.concatenate([high, high], axis=1)
    return np.concatenate([upper, np.concatenate([low, np.zeros_like(low)], axis=1)], axis=0)


def section_tables():
    dm, _, jm, dj, sigma = node_tables()
    eye = np.eye(8)
    values = np.kron(jm, jm)[:, ROWS]
    along = [np.kron(dm, eye)[ROWS][:, ROWS], np.kron(eye, dm)[ROWS][:, ROWS]]
    slopes = np.concatenate(along, axis=0)
    js, ds = sigma[:, None] * jm, sigma[:, None] * dj
    back_12 = np.concatenate([np.kron(ds, js).T, np.kron(js, ds).T], axis=1)
    back_3 = np.kron(js, js).T
    div = np.concatenate([matrix.T for matrix in along], axis=1)
    tables = {"values": three(values), "slopes": three(slopes)}
    for part, rows in enumerate(PART_ROWS):
        tables["back_12", part] = stacked(back_12[rows])
        tables["back_3", part] = stacked(back_3[rows])
        tables["div", part] = stacked(part_rows(part, div))
    return {name: lane_tiles(table) for name, table in tables.items()}


EARLY = ["values", "slopes", ("back_12", 0), ("back_3", 0), ("div", 0)]
LATE = [("back_12", 1), ("back_3", 1), ("div", 1)]


class Packed:
    def __init__(self, names):
        tables = section_tables()
        self.array = np.concatenate([tables[name].reshape(-1, LANES) for name in names])
        self.places, start = {}, 0
        for name in names:
            self.places[name] = (start, tables[name].shape)
            start += tables[name].shape[0] * tables[name].shape[1]

    def get(self, ref, name):
        start, (tiles, rows, _) = self.places[name]
        return [ref[start + k * rows : start + (k + 1) * rows] for k in range(tiles)]


def wall_bases():
    dm, rho, jm, dj, sigma = node_tables()
    lane = np.arange(LANES)
    gauss = np.arange(24)
    forward_lanes = [lane % 12, (lane + LANES) % 12]
    blocks = [dm.T[:, lane % 8]]
    blocks += [jm.T[:, lanes] for lanes in forward_lanes]
    blocks[2] = np.where(lane < 64, blocks[2], 0.0)
    blocks += [(sigma[:, None] * matrix)[gauss % 12][:, lane % 8] for matrix in (jm, dj)]
    blocks += [dm[:, lane % 8]]
    rows = [np.asarray(part, np.float32) for block in blocks for part in halves(block)]
    rows.append(np.asarray(rho[:, None] * rho[None, lane % 8], np.float32))
    return np.concatenate(rows), [float(weight) for weight in rho]


def build_wall_tables(bases, z_forward, z_back, w, rho):
    row = lax.broadcasted_iota(jnp.int32, (8, LANES), 0)
    lane = lax.broadcasted_iota(jnp.int32, (8, LANES), 1)
    zero = jnp.zeros((8, LANES), F32)
    nothing = jnp.zeros((LANES, LANES), BF16)
    for t in range(6):
        kind, low = t // 2, t % 2
        element = (lane // 8, lane // 12, (lane + LANES) // 12)[kind]
        base = bases[8 * t : 8 * t + 8]
        table = [jnp.where(element == a, base, zero) for a in range(16)]
        table = jnp.concatenate(table, axis=0).astype(BF16)
        z_forward[t, :LANES] = table
        z_forward[t, LANES:] = nothing if low else table
    for kind in range(2):
        for low in range(2):
            start = 48 + 24 * (2 * kind + low)
            table = []
            for block in range(24):
                inside = row + 8 * block - 12 * (lane // 8)
                base = bases[start + 8 * (block % 3) : start + 8 * (block % 3) + 8]
                table.append(jnp.where((inside >= 0) & (inside < 12), base, zero))
            table = jnp.concatenate(table, axis=0).astype(BF16)
            z_back[low, LANES * kind : LANES * (kind + 1)] = table[:LANES]
            z_back[low, 256 + 64 * kind : 320 + 64 * kind] = table[LANES:]
    for low in range(2):
        base = bases[144 + 8 * low : 152 + 8 * low]
        table = [jnp.where(lane // 8 == a, base, zero) for a in range(16)]
        z_back[low, 384:] = jnp.concatenate(table, axis=0).astype(BF16)
    for x in range(8):
        w[8 * x : 8 * x + 8] = bases[160:168] * rho[ROWS[8 * x] // 8]


def split(values):
    high = values.astype(BF16)
    low = (values - high.astype(F32)).astype(BF16)
    return high, low


def dot(left, right):
    return jnp.dot(left, right, preferred_element_type=F32)


def wide(tiles, columns=None):
    count = len(tiles) if isinstance(tiles, list) else tiles.shape[0]
    whole = jnp.concatenate([tiles[k] for k in range(count)], axis=1)
    return whole if columns is None else whole[:, :columns]


def fold(values):
    return values[:, :LANES] + values[:, LANES : 2 * LANES]


def section_rows(block, e):
    planes = block.reshape(8, 2, 8, LANES)[:, e]
    planes = jnp.concatenate([planes[:1], planes[7:], planes[1:7]], axis=0)
    return planes.reshape(XY, LANES)


def tiles_at(ref, tiles, rows=slice(None)):
    return jnp.concatenate([ref[k, rows] for k in tiles], axis=1)


def columns(values, count):
    return [values[:, k * LANES : (k + 1) * LANES] for k in range(count)]


def wall_stage(rows_of, z_forward, xhl, js, vs=None):
    count = js.shape[1] // 3
    skip = 2 if vs is None else 0
    batches = [[(c, e) for c in range(3)] for e in range(2)]
    if count < 32:
        batches = [batches[0] + batches[1]]
    pieces = {}
    for first, batch in enumerate(batches):
        start = first * 3 * count
        for k, (c, e) in enumerate(batch):
            rows = slice(start + k * count, start + (k + 1) * count)
            high, low = split(rows_of(c, e))
            xhl[0, rows], xhl[1, rows] = high, low
            if vs is not None:
                for t, part in enumerate((high, low, high)):
                    vs[2 * c + e, t * count : (t + 1) * count] = part
        out = dot(wide(xhl.at[:, start : start + len(batch) * count]), wide(z_forward.at[skip:]))
        for k, (c, e) in enumerate(batch):
            for kind in range(skip // 2, 3):
                lanes = slice((2 * kind - skip) * LANES, (2 * kind - skip + 2) * LANES)
                pieces[kind, c, e] = fold(out[k * count : (k + 1) * count, lanes])
    for c in range(3):
        tiles = [pieces[1, c, 0], pieces[1, c, 1]]
        tiles.append(pieces[2, c, 0] + pltpu.roll(pieces[2, c, 1], 64, 1))
        for t, tile in enumerate(tiles):
            high, low = split(tile)
            for k, part in enumerate((high, low, high)):
                js[3 * c + t, k * count : (k + 1) * count] = part
    return {(c, e): pieces[0, c, e] for c in range(3) for e in range(2)} if vs is not None else None


def right_side(refs, tiles):
    whole = []
    for k in tiles:
        parts = []
        for third in range(3):
            for ref in refs:
                count = ref.shape[1] // 3
                parts.append(ref[k, third * count : (third + 1) * count])
        whole.append(jnp.concatenate(parts, axis=0))
    return jnp.concatenate(whole, axis=1)


def at_gauss(jj, js, pair):
    return columns(dot(wide(jj, 3 * XY), right_side(js, pair)), len(pair))


def section_slopes(grads, vs, c):
    return columns(dot(wide(grads, 3 * XY), right_side(vs, (2 * c, 2 * c + 1))), 2)


def fine_flow(jj, js, u_ref):
    for pair in PAIRS:
        for k, tile in zip(pair, at_gauss(jj, js, pair)):
            u_ref[k] = tile


def front(slopes, jj, grads, js, vs, u_ref, metric, kept):
    ts, hs, h3s = kept

    def flux(c):
        for e, both in enumerate(section_slopes(grads, vs, c)):
            g1, g2, g3 = both[:XY], both[XY:], slopes[c, e]
            m11, m22, m33, m12, m13, m23 = (metric[k, e] for k in range(6))
            h1 = m11 * g1 + m12 * g2 + m13 * g3
            h2 = m12 * g1 + m22 * g2 + m23 * g3
            h3 = m13 * g1 + m23 * g2 + m33 * g3
            h1h, h1l = split(h1)
            h2h, h2l = split(h2)
            for k, part in enumerate((h1h, h2h, h1l, h2l)):
                hs[2 * c + e, k * XY : (k + 1) * XY] = part
            h3s[2 * c + e] = h3

    def gauss(pair):
        for k, tile in zip(pair, at_gauss(jj, js, pair)):
            for d in range(3):
                start = (0, QQ, 4 * QQ)[d]
                gap = (2 * QQ, 2 * QQ, QQ)[d]
                high, low = split(u_ref[3 * d + k % 3] * tile)
                ts[k, start : start + QQ] = high
                ts[k, start + gap : start + gap + QQ] = low

    if len(js) == 1:
        work = [(gauss, pair) for pair in PAIRS] + [(flux, c) for c in range(3)]
    else:
        work = [step for c in range(3) for step in ((gauss, PAIRS[c]), (flux, c))]
        work += [(gauss, pair) for pair in PAIRS[3:]]
    for step, argument in work:
        step(argument)


def back(part, tables, scratch, kept):
    z_back, back_12, back_3, div = tables
    ts, hs, h3s = kept
    bz = scratch["bz"]
    planes = PART_PLANES[part]
    count = 8 * len(planes)
    result = [[None, None] for _ in range(3)]
    sides = [{}, {}]
    for pair in PAIRS:
        for k, (table, depth, where) in enumerate(
            ((back_12, 4 * QQ, slice(0, 4 * QQ)), (back_3, 2 * QQ, slice(4 * QQ, None)))
        ):
            both = dot(wide(table, depth), tiles_at(ts, pair, where))
            both = both[:count] + both[count:]
            for tile, values in zip(pair, columns(both, len(pair))):
                sides[k][tile] = values
    spreads = dot(wide(div), tiles_at(hs, range(6)))
    spreads = columns(spreads[:count] + spreads[count:], 6)
    low_lanes = lax.broadcasted_iota(jnp.int32, (count, LANES), 1) < 64
    for c in range(3):
        spread = spreads[2 * c : 2 * c + 2]
        far = [sides[k][3 * c + 2] for k in range(2)]
        turned = [pltpu.roll(tile, 64, 1) for tile in far]
        far = [
            jnp.where(low_lanes, far[0], turned[1]),
            jnp.where(low_lanes, turned[0], far[1]),
        ]
        for e in range(2):
            result[c][e] = spread[e]
            rows = slice((2 * c + e) * count, (2 * c + e + 1) * count)
            near = [sides[k][3 * c + e] for k in range(2)]
            tiles = near + [far[e], part_rows(part, h3s[2 * c + e])]
            for t, tile in enumerate(tiles):
                bz[t, rows], bz[4 + t, rows] = split(tile)
    out = fold(dot(wide(bz.at[:4]), wide(z_back))) + dot(wide(bz.at[4:]), z_back[0])
    for c in range(3):
        for e in range(2):
            result[c][e] += out[(2 * c + e) * count : (2 * c + e + 1) * count]
    return result


def sum_local(pair, out_ref, slot):
    shape = (out_ref.shape[1], 8, LANES)
    row = lax.broadcasted_iota(jnp.int32, shape, 1)
    lane = lax.broadcasted_iota(jnp.int32, shape, 2)
    inner = lane % 8
    for e in range(2):
        mine = pair[e].reshape(shape)
        other = pair[1 - e].reshape(shape)
        total = mine + jnp.where(row == 7, pltpu.roll(other, 7, 1), 0.0)
        total = total + jnp.where(row == 0, pltpu.roll(other, 1, 1), 0.0)
        after = pltpu.roll(total, LANES - 1, 2)
        before = pltpu.roll(total, 1, 2)
        total = (
            total
            + jnp.where((inner == 7) & (lane < LANES - 1), after, 0.0)
            + jnp.where((inner == 0) & (lane > 0), before, 0.0)
        )
        out_ref[slot, :, 8 * e : 8 * (e + 1), :] = total


def positions():
    c = lax.axis_index("col")
    return c % 2, c == 0, c == lax.axis_size("col") - 1


def places(ref):
    fields, planes = ref.shape[:2]
    return [
        (slot, x, e, (slot * planes + x) * 2 + e)
        for slot in range(fields)
        for x in range(planes)
        for e in range(2)
    ]


def pack_edges(sum_ref, edge_ref):
    lane = lax.broadcasted_iota(jnp.int32, (8, LANES), 1)
    packed = jnp.zeros((8, LANES), F32)
    for slot, x, e, at in places(sum_ref):
        tile = sum_ref[slot, x, 8 * e : 8 * (e + 1), :]
        packed = jnp.where(lane == 2 * at, pltpu.roll(tile, 2 * at, 1) if at else tile, packed)
        packed = jnp.where(lane == 2 * at + 1, pltpu.roll(tile, (2 * at + 2) % LANES, 1), packed)
    edge_ref[...] = packed


def with_edges(sum_ref, edge_refs):
    col_odd, _, _ = positions()
    lane = lax.broadcasted_iota(jnp.int32, (8, LANES), 1)
    edges = jnp.zeros((8, LANES), F32)
    for k, ref in enumerate(edge_refs):
        edges = edges + jnp.where(lane % 2 == (col_odd + k) % 2, ref[...], 0.0)
    meets = (lane == LANES - 1) | (lane == 0)
    return {
        (slot, x, e): sum_ref[slot, x, 8 * e : 8 * (e + 1), :]
        + jnp.where(meets, pltpu.roll(edges, LANES - 1 - 2 * at, 1), 0.0)
        for slot, x, e, at in places(sum_ref)
    }


def planes_kernel(count, *refs):
    outer, edge_refs, (up, down) = refs[0], refs[1 : 1 + count], refs[-2:]
    for (slot, x, e), tile in with_edges(outer, edge_refs).items():
        (up if x else down)[slot, 8 * e : 8 * (e + 1), :] = tile


def arrived(own_refs, up_ref, down_ref):
    up, down = own_refs
    return {
        (slot, x, e): (up if x else down)[slot, 8 * e : 8 * (e + 1), :]
        + (down_ref if x else up_ref)[slot, 8 * e : 8 * (e + 1), :]
        for slot, x, e, _ in places(jax.ShapeDtypeStruct((up.shape[0], 2, 16, LANES), F32))
    }


def interior_mask():
    _, first, last = positions()
    lane = lax.broadcasted_iota(jnp.int32, (1, LANES), 1)
    outer = ((lane == 0) & first) | ((lane == LANES - 1) & last)
    return jnp.where(outer, 0.0, 1.0)


def scale_metric(diag_ref, cross_ref, weights, metric):
    for k in range(6):
        ref = diag_ref if k < 3 else cross_ref
        block = ref[k % 3].astype(F32)
        for e in range(2):
            metric[k, e] = section_rows(block, e) * weights[...] * VISCOSITY


def finish(part, kept, tables, scratch, total, edge, mass=None):
    result = back(part, tables, scratch, kept)
    for c in range(3):
        sum_local(result[c], total, c)
    if mass is not None:
        jac, w = mass
        rows = [part_rows(part, section_rows(jac[...], e) * w[...]) for e in range(2)]
        sum_local(rows, total, 3)
    pack_edges(total, edge)


def back_tables(z_back, packed, ref, part):
    return [z_back] + [packed.get(ref, (kind, part)) for kind in ("back_12", "back_3", "div")]


def first_kernel(early_pack, rho, *refs):
    sources, refs = refs[:8], refs[8:]
    v, early, late, z_forward, z_back, jac, w, u, metric, *kept = refs[:12]
    total, edge, bases, b, gd, gc, sems = refs[12:19]
    bz, xhl, js, vs, flow_xhl, flow_js = refs[19:]
    targets = [bases, b, v, early, gd, gc, jac, late]
    copies = [
        pltpu.make_async_copy(source, target, sems.at[k])
        for k, (source, target) in enumerate(zip(sources, targets))
    ]
    for copy in copies:
        copy.start()
    copies[0].wait()
    build_wall_tables(bases, z_forward, z_back, w, rho)
    copies[1].wait()
    copies[2].wait()
    wall_stage(lambda c, e: section_rows(b[c], e), z_forward, flow_xhl, flow_js)
    by_wall = wall_stage(lambda c, e: section_rows(v[c], e), z_forward, xhl, js, vs)
    copies[3].wait()
    copies[4].wait()
    copies[5].wait()
    copies[6].wait()
    values, slopes = early_pack.get(early, "values"), early_pack.get(early, "slopes")
    fine_flow(values, [flow_js], u)
    scale_metric(gd, gc, w, metric)
    front(by_wall, values, slopes, [js], [vs], u, metric, kept)
    tables = back_tables(z_back, early_pack, early, 0)
    finish(0, kept, tables, {"bz": bz}, total, edge, (jac, w))
    copies[7].wait()


def inner_kernel(has_mass, late_pack, *refs):
    kept, (z_back, late), refs = refs[:3], refs[3:5], refs[5:]
    mass, refs = (refs[:2], refs[2:]) if has_mass else (None, refs)
    total, edge, bz = refs
    tables = back_tables(z_back, late_pack, late, 1)
    finish(1, kept, tables, {"bz": bz}, total, edge, mass)


def half_step(part, tiles, v, inverse, half):
    mask = interior_mask()
    for k, x in enumerate(PART_PLANES[part]):
        for e in range(2):
            rows = slice(8 * e, 8 * (e + 1))
            inv = 1.0 / tiles[3, k, e]
            inverse[k, rows] = inv
            for c in range(3):
                step = (0.5 * STEP_SIZE) * inv * tiles[c, k, e]
                half[c, e, 8 * k : 8 * (k + 1)] = mask * (v[c, x, rows] - step)


def prepare_kernel(edges, *refs):
    v, z_forward, summed = refs[:3]
    inverse, js, vs, wall_slopes, half, xhl = refs[3 + edges :]
    half_step(1, with_edges(summed, refs[3 : 3 + edges]), v, inverse, half)
    by_wall = wall_stage(lambda c, e: half[c, e], z_forward, xhl, js, vs)
    for (c, e), slope in by_wall.items():
        wall_slopes[2 * c + e] = slope


def second_kernel(early_pack, *refs):
    v, z_forward, z_back, early, u, metric = refs[:6]
    inner_js, inner_vs, wall_slopes, up, down, up_in, down_in = refs[6:13]
    inverse, kept, (total, edge) = refs[13], refs[14:17], refs[17:19]
    bz, xhl, js, vs, half = refs[19:]
    values, slopes = early_pack.get(early, "values"), early_pack.get(early, "slopes")
    half_step(0, arrived((up, down), up_in, down_in), v, inverse, half)
    by_wall = wall_stage(lambda c, e: half[c, e], z_forward, xhl, js, vs)
    for c, e in by_wall:
        by_wall[c, e] = jnp.concatenate([by_wall[c, e], wall_slopes[2 * c + e]], axis=0)
    front(by_wall, values, slopes, [js, inner_js], [vs, inner_vs], u, metric, kept)
    tables = back_tables(z_back, early_pack, early, 0)
    finish(0, kept, tables, {"bz": bz}, total, edge)


def advance(part, tiles, v, inverse, held):
    mask = interior_mask()
    planes = PART_PLANES[part]
    for c in range(3):
        for k, x in enumerate(planes):
            for e in range(2):
                rows = slice(8 * e, 8 * (e + 1))
                step = STEP_SIZE * inverse[k, rows] * tiles[c, k, e]
                held[c, k, rows] = mask * (v[c, x, rows] - step)


def advance_inner_kernel(edges, *refs):
    v, inverse, summed = refs[:3]
    advance(1, with_edges(summed, refs[3 : 3 + edges]), v, inverse, refs[-1])


def advance_kernel(*refs):
    v, inverse, inner, up, down, up_in, down_in, out, held, sems = refs
    copies = [pltpu.make_async_copy(inner, out.at[:, 1:7], sems.at[0])]
    copies[0].start()
    advance(0, arrived((up, down), up_in, down_in), v, inverse, held)
    for k, x in enumerate(PART_PLANES[0]):
        copies.append(pltpu.make_async_copy(held.at[:, k], out.at[:, x], sems.at[1 + k]))
        copies[-1].start()
    for copy in copies:
        copy.wait()


def back_scratch(part):
    return [pltpu.VMEM((8, 6 * 8 * len(PART_PLANES[part]), LANES), BF16)]


def front_scratch(count, with_field=True):
    shapes = [(2, 6 * count, LANES), (9, 3 * count, LANES), (6, 3 * count, LANES)]
    return [pltpu.VMEM(shape, BF16) for shape in shapes[: 3 if with_field else 2]]


def call(kernel, name, ins, outs, scratch, in_space=pltpu.VMEM, out_space=pltpu.VMEM):
    ins = [pltpu.with_memory_space_constraint(array, in_space) for array in ins]
    return pl.pallas_call(
        kernel,
        name=name,
        out_shape=[out_space(shape, dtype) for shape, dtype in outs],
        in_specs=[pl.BlockSpec(memory_space=in_space)] * len(ins),
        out_specs=[pl.BlockSpec(memory_space=out_space)] * len(outs),
        scratch_shapes=scratch,
        compiler_params=pltpu.CompilerParams(vmem_limit_bytes=24 * 1024 * 1024),
    )(*ins)


def wall_pairings(count):
    even = [(i, i + 1) for i in range(0, count - 1, 2)]
    odd = [(i, i + 1) for i in range(1, count - 1, 2)]
    return [pairs + [(b, a) for a, b in pairs] for pairs in (even, odd) if pairs]


def swap_edges(edge):
    return [lax.ppermute(edge, "col", way) for way in wall_pairings(lax.axis_size("col"))]


def local(adjoint_field, base_flow, metric_diag, metric_cross, jacobian):
    early_pack, late_pack = Packed(EARLY), Packed(LATE)
    bases, rho = wall_bases()
    block = adjoint_field.shape[1:]
    field = ((3,) + block, F32)
    kept_shapes = [
        ((9, 6 * QQ, LANES), BF16),
        ((6, 4 * XY, LANES), BF16),
        ((6, XY, LANES), F32),
    ]
    edge_shape = ((8, LANES), F32)
    spans = lax.axis_size("span")
    ahead = [(i, (i + 1) % spans) for i in range(spans)]
    back_way = [(b, a) for a, b in ahead]

    def sums(fields, part):
        return [((fields, len(PART_PLANES[part])) + block[1:], F32), edge_shape]

    def exchange(fields, outer, outer_edge, operands):
        outer_edges = swap_edges(outer_edge)
        inner, inner_edge = call(
            functools.partial(inner_kernel, len(operands) > 5, late_pack),
            "inner_planes",
            operands,
            sums(fields, 1),
            back_scratch(1),
        )
        up, down = call(
            functools.partial(planes_kernel, len(outer_edges)),
            "planes",
            [outer] + outer_edges + [inner_edge],
            [((fields,) + block[1:], F32)] * 2,
            [],
        )
        inner_edges = swap_edges(inner_edge)
        up_in, down_in = lax.ppermute(up, "span", ahead), lax.ppermute(down, "span", back_way)
        return [up, down, up_in, down_in], inner, inner_edges

    early, late = (jnp.asarray(pack.array, BF16) for pack in (early_pack, late_pack))
    ins = [jnp.asarray(bases), base_flow, adjoint_field, early]
    ins += [metric_diag, metric_cross, jacobian, late]
    v, early, late, z_forward, z_back, jac, w, u, metric, *kept, outer, outer_edge = call(
        functools.partial(first_kernel, early_pack, rho),
        "first_operator",
        ins,
        [field, (early.shape, BF16), (late.shape, BF16)]
        + [((6, 2 * LANES, LANES), BF16), ((2, 512, LANES), BF16)]
        + [(block, F32), ((XY, LANES), F32)]
        + [((9, QQ, LANES), F32), ((6, 2, XY, LANES), F32)]
        + kept_shapes
        + sums(4, 0),
        [
            pltpu.VMEM(bases.shape, F32),
            pltpu.VMEM((3,) + block, F32),
            pltpu.VMEM((3,) + block, BF16),
            pltpu.VMEM((3,) + block, BF16),
            pltpu.SemaphoreType.DMA((len(ins),)),
        ]
        + back_scratch(0)
        + front_scratch(XY)
        + front_scratch(XY, False),
        in_space=pltpu.HBM,
    )
    planes, inner, inner_edges = exchange(4, outer, outer_edge, kept + [z_back, late, jac, w])
    half = [pltpu.VMEM((3, 2, 8 * len(planes), LANES), F32) for planes in PART_PLANES]
    inner_inverse, *prepared = call(
        functools.partial(prepare_kernel, len(inner_edges)),
        "prepare",
        [v, z_forward, inner] + inner_edges,
        [
            ((6,) + block[1:], F32),
            ((9, 144, LANES), BF16),
            ((6, 144, LANES), BF16),
            ((6, 48, LANES), F32),
        ],
        [half[1], front_scratch(48)[0]],
    )
    inverse, *kept, outer, outer_edge = call(
        functools.partial(second_kernel, early_pack),
        "second_operator",
        [v, z_forward, z_back, early, u, metric] + prepared + planes,
        [((2,) + block[1:], F32)] + kept_shapes + sums(3, 0),
        back_scratch(0) + front_scratch(16) + [half[0]],
    )
    planes, inner, inner_edges = exchange(3, outer, outer_edge, kept + [z_back, late])
    (done,) = call(
        functools.partial(advance_inner_kernel, len(inner_edges)),
        "advance_inner",
        [v, inner_inverse, inner] + inner_edges,
        [((3, 6) + block[1:], F32)],
        [],
    )
    (out,) = call(
        advance_kernel,
        "advance",
        [v, inverse, done] + planes,
        [field],
        [pltpu.VMEM((3, 2) + block[1:], F32), pltpu.SemaphoreType.DMA((3,))],
        out_space=pltpu.HBM,
    )
    return out


def solution(mesh):
    in_specs = (
        P(None, "span", None, "col"),
        P(None, "span", None, "col"),
        P(None, "span", None, "col"),
        P(None, "span", None, "col"),
        P("span", None, "col"),
    )
    out_specs = P(None, "span", None, "col")
    return jax.shard_map(local, mesh=mesh, in_specs=in_specs, out_specs=out_specs, check_vma=False)
```

```python
import functools

import jax
import jax.numpy as jnp
import numpy as np
from jax import lax
from jax.experimental import pallas as pl
from jax.experimental.pallas import tpu as pltpu
from jax.sharding import PartitionSpec as P

VISCOSITY = 0.05
STEP_SIZE = 0.01
GLL_INNER = [
    -0.8717401485096066,
    -0.5917001814331423,
    -0.2092992179024789,
    0.2092992179024789,
    0.5917001814331423,
    0.8717401485096066,
]
GAUSS_POINTS = [
    -0.9815606342467192,
    -0.9041172563704749,
    -0.7699026741943047,
    -0.5873179542866175,
    -0.3678314989981802,
    -0.1252334085114689,
    0.1252334085114689,
    0.3678314989981802,
    0.5873179542866175,
    0.7699026741943047,
    0.9041172563704749,
    0.9815606342467192,
]
GAUSS_WEIGHTS = [
    0.0471753363865118,
    0.1069393259953184,
    0.1600783285433462,
    0.2031674267230659,
    0.2334925365383548,
    0.2491470458134028,
    0.2491470458134028,
    0.2334925365383548,
    0.2031674267230659,
    0.1600783285433462,
    0.1069393259953184,
    0.0471753363865118,
]
F32 = jnp.float32
BF16 = jnp.bfloat16
XY = 64
QQ = 144
LANES = 128
PART_PLANES = ([0, 7], [1, 2, 3, 4, 5, 6])
PART_ROWS = [[8 * x + y for x in planes for y in range(8)] for planes in PART_PLANES]
ROWS = PART_ROWS[0] + PART_ROWS[1]
PAIRS = [(0, 1), (2, 3), (4, 5), (6, 7), (8,)]


def legendre_seven(points):
    previous = points * 0.0 + 1.0
    current = points
    for degree in range(1, 7):
        following = ((2.0 * degree + 1.0) * points * current - degree * previous) / (degree + 1.0)
        previous = current
        current = following
    return current


def node_tables():
    gll_nodes = np.array([-1.0] + GLL_INNER + [1.0])
    values = legendre_seven(gll_nodes)
    node_weights = 2.0 / (56.0 * values * values)
    identity = np.eye(8, dtype=bool)
    spacing = gll_nodes[:, None] - gll_nodes[None, :]
    derivative = np.where(
        identity, 0.0, values[:, None] / (values[None, :] * np.where(identity, 1.0, spacing))
    )
    corner_terms = np.concatenate([np.array([-14.0]), np.zeros(6), np.array([14.0])])
    derivative = derivative + np.eye(8) * corner_terms[None, :]
    gauss_nodes = np.array(GAUSS_POINTS)
    gauss_weights = np.array(GAUSS_WEIGHTS)
    numerators = gauss_nodes[:, None, None] - gll_nodes[None, None, :]
    denominators = np.where(identity, 1.0, spacing)[None]
    ratios = np.where(identity[None], 1.0, numerators / denominators)
    interpolation = ratios.prod(axis=2)
    slope_interp = interpolation @ derivative
    return (derivative, node_weights, interpolation, slope_interp, gauss_weights)


def halves(matrix):
    high = np.asarray(matrix, np.float32).astype(jnp.bfloat16)
    low = (np.asarray(matrix, np.float64) - high.astype(np.float64)).astype(jnp.bfloat16)
    return high, low


def lane_tiles(table):
    rows, columns = table.shape
    padded = np.pad(table, ((0, 0), (0, -columns % LANES)))
    return padded.reshape(rows, -1, LANES).transpose(1, 0, 2)


def part_rows(part, tall):
    return tall[16:] if part else tall[:16]


def three(matrix):
    high, low = halves(matrix)
    return np.concatenate([high, high, low], axis=1)


def stacked(matrix):
    high, low = halves(matrix)
    upper = np.concatenate([high, high], axis=1)
    return np.concatenate([upper, np.concatenate([low, np.zeros_like(low)], axis=1)], axis=0)


def section_tables():
    dm, _, jm, dj, sigma = node_tables()
    eye = np.eye(8)
    values = np.kron(jm, jm)[:, ROWS]
    along = [np.kron(dm, eye)[ROWS][:, ROWS], np.kron(eye, dm)[ROWS][:, ROWS]]
    slopes = np.concatenate(along, axis=0)
    js, ds = sigma[:, None] * jm, sigma[:, None] * dj
    back_12 = np.concatenate([np.kron(ds, js).T, np.kron(js, ds).T], axis=1)
    back_3 = np.kron(js, js).T
    div = np.concatenate([matrix.T for matrix in along], axis=1)
    tables = {"values": three(values), "slopes": three(slopes)}
    for part, rows in enumerate(PART_ROWS):
        tables["back_12", part] = stacked(back_12[rows])
        tables["back_3", part] = stacked(back_3[rows])
        tables["div", part] = stacked(part_rows(part, div))
    return {name: lane_tiles(table) for name, table in tables.items()}


EARLY = ["values", "slopes", ("back_12", 0), ("back_3", 0), ("div", 0)]
LATE = [("back_12", 1), ("back_3", 1), ("div", 1)]


class Packed:
    def __init__(self, names):
        tables = section_tables()
        self.array = np.concatenate([tables[name].reshape(-1, LANES) for name in names])
        self.places, start = {}, 0
        for name in names:
            self.places[name] = (start, tables[name].shape)
            start += tables[name].shape[0] * tables[name].shape[1]

    def get(self, ref, name):
        start, (tiles, rows, _) = self.places[name]
        return [ref[start + k * rows : start + (k + 1) * rows] for k in range(tiles)]


def wall_bases():
    dm, rho, jm, dj, sigma = node_tables()
    lane = np.arange(LANES)
    gauss = np.arange(24)
    forward_lanes = [lane % 12, (lane + LANES) % 12]
    blocks = [dm.T[:, lane % 8]]
    blocks += [jm.T[:, lanes] for lanes in forward_lanes]
    blocks[2] = np.where(lane < 64, blocks[2], 0.0)
    blocks += [(sigma[:, None] * matrix)[gauss % 12][:, lane % 8] for matrix in (jm, dj)]
    blocks += [dm[:, lane % 8]]
    rows = [np.asarray(part, np.float32) for block in blocks for part in halves(block)]
    rows.append(np.asarray(rho[:, None] * rho[None, lane % 8], np.float32))
    return np.concatenate(rows), [float(weight) for weight in rho]


def build_wall_tables(bases, z_forward, z_back, w, rho):
    row = lax.broadcasted_iota(jnp.int32, (8, LANES), 0)
    lane = lax.broadcasted_iota(jnp.int32, (8, LANES), 1)
    zero = jnp.zeros((8, LANES), F32)
    nothing = jnp.zeros((LANES, LANES), BF16)
    for t in range(6):
        kind, low = t // 2, t % 2
        element = (lane // 8, lane // 12, (lane + LANES) // 12)[kind]
        base = bases[8 * t : 8 * t + 8]
        table = [jnp.where(element == a, base, zero) for a in range(16)]
        table = jnp.concatenate(table, axis=0).astype(BF16)
        z_forward[t, :LANES] = table
        z_forward[t, LANES:] = nothing if low else table
    for kind in range(2):
        for low in range(2):
            start = 48 + 24 * (2 * kind + low)
            table = []
            for block in range(24):
                inside = row + 8 * block - 12 * (lane // 8)
                base = bases[start + 8 * (block % 3) : start + 8 * (block % 3) + 8]
                table.append(jnp.where((inside >= 0) & (inside < 12), base, zero))
            table = jnp.concatenate(table, axis=0).astype(BF16)
            z_back[low, LANES * kind : LANES * (kind + 1)] = table[:LANES]
            z_back[low, 256 + 64 * kind : 320 + 64 * kind] = table[LANES:]
    for low in range(2):
        base = bases[144 + 8 * low : 152 + 8 * low]
        table = [jnp.where(lane // 8 == a, base, zero) for a in range(16)]
        z_back[low, 384:] = jnp.concatenate(table, axis=0).astype(BF16)
    for x in range(8):
        w[8 * x : 8 * x + 8] = bases[160:168] * rho[ROWS[8 * x] // 8]


def split(values):
    high = values.astype(BF16)
    low = (values - high.astype(F32)).astype(BF16)
    return high, low


def dot(left, right):
    return jnp.dot(left, right, preferred_element_type=F32)


def wide(tiles, columns=None):
    count = len(tiles) if isinstance(tiles, list) else tiles.shape[0]
    whole = jnp.concatenate([tiles[k] for k in range(count)], axis=1)
    return whole if columns is None else whole[:, :columns]


def fold(values):
    return values[:, :LANES] + values[:, LANES : 2 * LANES]


def section_rows(block, e):
    planes = block.reshape(8, 2, 8, LANES)[:, e]
    planes = jnp.concatenate([planes[:1], planes[7:], planes[1:7]], axis=0)
    return planes.reshape(XY, LANES)


def tiles_at(ref, tiles, rows=slice(None)):
    return jnp.concatenate([ref[k, rows] for k in tiles], axis=1)


def columns(values, count):
    return [values[:, k * LANES : (k + 1) * LANES] for k in range(count)]


def wall_stage(rows_of, z_forward, xhl, js, vs=None):
    count = js.shape[1] // 3
    skip = 2 if vs is None else 0
    batches = [[(c, e) for c in range(3)] for e in range(2)]
    if count < 32:
        batches = [batches[0] + batches[1]]
    pieces = {}
    for first, batch in enumerate(batches):
        start = first * 3 * count
        for k, (c, e) in enumerate(batch):
            rows = slice(start + k * count, start + (k + 1) * count)
            high, low = split(rows_of(c, e))
            xhl[0, rows], xhl[1, rows] = high, low
            if vs is not None:
                for t, part in enumerate((high, low, high)):
                    vs[2 * c + e, t * count : (t + 1) * count] = part
        out = dot(wide(xhl.at[:, start : start + len(batch) * count]), wide(z_forward.at[skip:]))
        for k, (c, e) in enumerate(batch):
            for kind in range(skip // 2, 3):
                lanes = slice((2 * kind - skip) * LANES, (2 * kind - skip + 2) * LANES)
                pieces[kind, c, e] = fold(out[k * count : (k + 1) * count, lanes])
    for c in range(3):
        tiles = [pieces[1, c, 0], pieces[1, c, 1]]
        tiles.append(pieces[2, c, 0] + pltpu.roll(pieces[2, c, 1], 64, 1))
        for t, tile in enumerate(tiles):
            high, low = split(tile)
            for k, part in enumerate((high, low, high)):
                js[3 * c + t, k * count : (k + 1) * count] = part
    return {(c, e): pieces[0, c, e] for c in range(3) for e in range(2)} if vs is not None else None


def right_side(refs, tiles):
    whole = []
    for k in tiles:
        parts = []
        for third in range(3):
            for ref in refs:
                count = ref.shape[1] // 3
                parts.append(ref[k, third * count : (third + 1) * count])
        whole.append(jnp.concatenate(parts, axis=0))
    return jnp.concatenate(whole, axis=1)


def at_gauss(jj, js, pair):
    return columns(dot(wide(jj, 3 * XY), right_side(js, pair)), len(pair))


def section_slopes(grads, vs, c):
    return columns(dot(wide(grads, 3 * XY), right_side(vs, (2 * c, 2 * c + 1))), 2)


def fine_flow(jj, js, u_ref):
    for pair in PAIRS:
        for k, tile in zip(pair, at_gauss(jj, js, pair)):
            u_ref[k] = tile


def front(slopes, jj, grads, js, vs, u_ref, metric, kept):
    ts, hs, h3s = kept

    def flux(c):
        for e, both in enumerate(section_slopes(grads, vs, c)):
            g1, g2, g3 = both[:XY], both[XY:], slopes[c, e]
            m11, m22, m33, m12, m13, m23 = (metric[k, e] for k in range(6))
            h1 = m11 * g1 + m12 * g2 + m13 * g3
            h2 = m12 * g1 + m22 * g2 + m23 * g3
            h3 = m13 * g1 + m23 * g2 + m33 * g3
            h1h, h1l = split(h1)
            h2h, h2l = split(h2)
            for k, part in enumerate((h1h, h2h, h1l, h2l)):
                hs[2 * c + e, k * XY : (k + 1) * XY] = part
            h3s[2 * c + e] = h3

    def gauss(pair):
        for k, tile in zip(pair, at_gauss(jj, js, pair)):
            for d in range(3):
                start = (0, QQ, 4 * QQ)[d]
                gap = (2 * QQ, 2 * QQ, QQ)[d]
                high, low = split(u_ref[3 * d + k % 3] * tile)
                ts[k, start : start + QQ] = high
                ts[k, start + gap : start + gap + QQ] = low

    if len(js) == 1:
        work = [(gauss, pair) for pair in PAIRS] + [(flux, c) for c in range(3)]
    else:
        work = [step for c in range(3) for step in ((gauss, PAIRS[c]), (flux, c))]
        work += [(gauss, pair) for pair in PAIRS[3:]]
    for step, argument in work:
        step(argument)


def back(part, tables, scratch, kept):
    z_back, back_12, back_3, div = tables
    ts, hs, h3s = kept
    bz = scratch["bz"]
    planes = PART_PLANES[part]
    count = 8 * len(planes)
    result = [[None, None] for _ in range(3)]
    sides = [{}, {}]
    for pair in PAIRS:
        for k, (table, depth, where) in enumerate(
            ((back_12, 4 * QQ, slice(0, 4 * QQ)), (back_3, 2 * QQ, slice(4 * QQ, None)))
        ):
            both = dot(wide(table, depth), tiles_at(ts, pair, where))
            both = both[:count] + both[count:]
            for tile, values in zip(pair, columns(both, len(pair))):
                sides[k][tile] = values
    spreads = dot(wide(div), tiles_at(hs, range(6)))
    spreads = columns(spreads[:count] + spreads[count:], 6)
    low_lanes = lax.broadcasted_iota(jnp.int32, (count, LANES), 1) < 64
    for c in range(3):
        spread = spreads[2 * c : 2 * c + 2]
        far = [sides[k][3 * c + 2] for k in range(2)]
        turned = [pltpu.roll(tile, 64, 1) for tile in far]
        far = [
            jnp.where(low_lanes, far[0], turned[1]),
            jnp.where(low_lanes, turned[0], far[1]),
        ]
        for e in range(2):
            result[c][e] = spread[e]
            rows = slice((2 * c + e) * count, (2 * c + e + 1) * count)
            near = [sides[k][3 * c + e] for k in range(2)]
            tiles = near + [far[e], part_rows(part, h3s[2 * c + e])]
            for t, tile in enumerate(tiles):
                bz[t, rows], bz[4 + t, rows] = split(tile)
    out = fold(dot(wide(bz.at[:4]), wide(z_back))) + dot(wide(bz.at[4:]), z_back[0])
    for c in range(3):
        for e in range(2):
            result[c][e] += out[(2 * c + e) * count : (2 * c + e + 1) * count]
    return result


def sum_local(pair, out_ref, slot):
    shape = (out_ref.shape[1], 8, LANES)
    row = lax.broadcasted_iota(jnp.int32, shape, 1)
    lane = lax.broadcasted_iota(jnp.int32, shape, 2)
    inner = lane % 8
    for e in range(2):
        mine = pair[e].reshape(shape)
        other = pair[1 - e].reshape(shape)
        total = mine + jnp.where(row == 7, pltpu.roll(other, 7, 1), 0.0)
        total = total + jnp.where(row == 0, pltpu.roll(other, 1, 1), 0.0)
        after = pltpu.roll(total, LANES - 1, 2)
        before = pltpu.roll(total, 1, 2)
        total = (
            total
            + jnp.where((inner == 7) & (lane < LANES - 1), after, 0.0)
            + jnp.where((inner == 0) & (lane > 0), before, 0.0)
        )
        out_ref[slot, :, 8 * e : 8 * (e + 1), :] = total


def positions():
    c = lax.axis_index("col")
    return c % 2, c == 0, c == lax.axis_size("col") - 1


def places(ref):
    fields, planes = ref.shape[:2]
    return [
        (slot, x, e, (slot * planes + x) * 2 + e)
        for slot in range(fields)
        for x in range(planes)
        for e in range(2)
    ]


def one_wall_neighbour():
    return len(wall_pairings(lax.axis_size("col"))) == 1


def pack_edges(sum_ref, edge_ref):
    lane = lax.broadcasted_iota(jnp.int32, (8, LANES), 1)
    packed = jnp.zeros((8, LANES), F32)
    alone = one_wall_neighbour()
    col_odd, _, _ = positions()
    for slot, x, e, at in places(sum_ref):
        tile = sum_ref[slot, x, 8 * e : 8 * (e + 1), :]
        if alone:
            packed = jnp.where(lane == at + 1, pltpu.roll(tile, at + 2 - col_odd, 1), packed)
        else:
            packed = jnp.where(lane == 2 * at, pltpu.roll(tile, 2 * at, 1) if at else tile, packed)
            last = pltpu.roll(tile, (2 * at + 2) % LANES, 1)
            packed = jnp.where(lane == 2 * at + 1, last, packed)
    edge_ref[...] = packed


def with_edges(sum_ref, edge_refs):
    col_odd, _, _ = positions()
    lane = lax.broadcasted_iota(jnp.int32, (8, LANES), 1)
    if one_wall_neighbour():
        edges = edge_refs[0][...]
        meets = lane == (LANES - 1) * (1 - col_odd)
    else:
        edges = jnp.zeros((8, LANES), F32)
        for k, ref in enumerate(edge_refs):
            edges = edges + jnp.where(lane % 2 == (col_odd + k) % 2, ref[...], 0.0)
        meets = (lane == LANES - 1) | (lane == 0)
    tiles = {}
    for slot, x, e, at in places(sum_ref):
        shift = LANES - 2 - at + col_odd if one_wall_neighbour() else LANES - 1 - 2 * at
        add = jnp.where(meets, pltpu.roll(edges, shift, 1), 0.0)
        tiles[slot, x, e] = sum_ref[slot, x, 8 * e : 8 * (e + 1), :] + add
    return tiles


def planes_kernel(count, *refs):
    outer, edge_refs, (up, down) = refs[0], refs[1 : 1 + count], refs[-2:]
    for (slot, x, e), tile in with_edges(outer, edge_refs).items():
        (up if x else down)[slot, 8 * e : 8 * (e + 1), :] = tile


def arrived(own_refs, up_ref, down_ref):
    up, down = own_refs
    return {
        (slot, x, e): (up if x else down)[slot, 8 * e : 8 * (e + 1), :]
        + (down_ref if x else up_ref)[slot, 8 * e : 8 * (e + 1), :]
        for slot, x, e, _ in places(jax.ShapeDtypeStruct((up.shape[0], 2, 16, LANES), F32))
    }


def interior_mask():
    _, first, last = positions()
    lane = lax.broadcasted_iota(jnp.int32, (1, LANES), 1)
    outer = ((lane == 0) & first) | ((lane == LANES - 1) & last)
    return jnp.where(outer, 0.0, 1.0)


def scale_metric(diag_ref, cross_ref, weights, metric):
    for k in range(6):
        ref = diag_ref if k < 3 else cross_ref
        block = ref[k % 3].astype(F32)
        for e in range(2):
            metric[k, e] = section_rows(block, e) * weights[...] * VISCOSITY


def finish(part, kept, tables, scratch, total, edge, mass=None):
    result = back(part, tables, scratch, kept)
    for c in range(3):
        sum_local(result[c], total, c)
    if mass is not None:
        jac, w = mass
        rows = [part_rows(part, section_rows(jac[...], e) * w[...]) for e in range(2)]
        sum_local(rows, total, 3)
    pack_edges(total, edge)


def back_tables(z_back, packed, ref, part):
    return [z_back] + [packed.get(ref, (kind, part)) for kind in ("back_12", "back_3", "div")]


def first_kernel(early_pack, rho, *refs):
    sources, refs = refs[:8], refs[8:]
    v, early, late, z_forward, z_back, jac, w, u, metric, *kept = refs[:12]
    total, edge, bases, b, gd, gc, sems = refs[12:19]
    bz, xhl, js, vs, flow_xhl, flow_js = refs[19:]
    targets = [bases, b, v, early, gd, gc, jac, late]
    copies = [
        pltpu.make_async_copy(source, target, sems.at[k])
        for k, (source, target) in enumerate(zip(sources, targets))
    ]
    for copy in copies:
        copy.start()
    copies[0].wait()
    build_wall_tables(bases, z_forward, z_back, w, rho)
    copies[1].wait()
    copies[2].wait()
    wall_stage(lambda c, e: section_rows(b[c], e), z_forward, flow_xhl, flow_js)
    by_wall = wall_stage(lambda c, e: section_rows(v[c], e), z_forward, xhl, js, vs)
    copies[3].wait()
    copies[4].wait()
    copies[5].wait()
    copies[6].wait()
    values, slopes = early_pack.get(early, "values"), early_pack.get(early, "slopes")
    fine_flow(values, [flow_js], u)
    scale_metric(gd, gc, w, metric)
    front(by_wall, values, slopes, [js], [vs], u, metric, kept)
    tables = back_tables(z_back, early_pack, early, 0)
    finish(0, kept, tables, {"bz": bz}, total, edge, (jac, w))
    copies[7].wait()


def inner_kernel(has_mass, late_pack, *refs):
    kept, (z_back, late), refs = refs[:3], refs[3:5], refs[5:]
    mass, refs = (refs[:2], refs[2:]) if has_mass else (None, refs)
    total, edge, bz = refs
    tables = back_tables(z_back, late_pack, late, 1)
    finish(1, kept, tables, {"bz": bz}, total, edge, mass)


def half_step(part, tiles, v, inverse, half):
    mask = interior_mask()
    for k, x in enumerate(PART_PLANES[part]):
        for e in range(2):
            rows = slice(8 * e, 8 * (e + 1))
            inv = 1.0 / tiles[3, k, e]
            inverse[k, rows] = inv
            for c in range(3):
                step = (0.5 * STEP_SIZE) * inv * tiles[c, k, e]
                half[c, e, 8 * k : 8 * (k + 1)] = mask * (v[c, x, rows] - step)


def prepare_kernel(edges, *refs):
    v, z_forward, summed = refs[:3]
    inverse, js, vs, wall_slopes, half, xhl = refs[3 + edges :]
    half_step(1, with_edges(summed, refs[3 : 3 + edges]), v, inverse, half)
    by_wall = wall_stage(lambda c, e: half[c, e], z_forward, xhl, js, vs)
    for (c, e), slope in by_wall.items():
        wall_slopes[2 * c + e] = slope


def second_kernel(early_pack, *refs):
    v, z_forward, z_back, early, u, metric = refs[:6]
    inner_js, inner_vs, wall_slopes, up, down, up_in, down_in = refs[6:13]
    inverse, kept, (total, edge) = refs[13], refs[14:17], refs[17:19]
    bz, xhl, js, vs, half = refs[19:]
    values, slopes = early_pack.get(early, "values"), early_pack.get(early, "slopes")
    half_step(0, arrived((up, down), up_in, down_in), v, inverse, half)
    by_wall = wall_stage(lambda c, e: half[c, e], z_forward, xhl, js, vs)
    for c, e in by_wall:
        by_wall[c, e] = jnp.concatenate([by_wall[c, e], wall_slopes[2 * c + e]], axis=0)
    front(by_wall, values, slopes, [js, inner_js], [vs, inner_vs], u, metric, kept)
    tables = back_tables(z_back, early_pack, early, 0)
    finish(0, kept, tables, {"bz": bz}, total, edge)


def advance(part, tiles, v, inverse, held):
    mask = interior_mask()
    planes = PART_PLANES[part]
    for c in range(3):
        for k, x in enumerate(planes):
            for e in range(2):
                rows = slice(8 * e, 8 * (e + 1))
                step = STEP_SIZE * inverse[k, rows] * tiles[c, k, e]
                held[c, k, rows] = mask * (v[c, x, rows] - step)


def advance_inner_kernel(edges, *refs):
    v, inverse, summed = refs[:3]
    advance(1, with_edges(summed, refs[3 : 3 + edges]), v, inverse, refs[-1])


def advance_kernel(*refs):
    v, inverse, inner, up, down, up_in, down_in, out, held, sems = refs
    copies = [pltpu.make_async_copy(inner, out.at[:, 1:7], sems.at[0])]
    copies[0].start()
    advance(0, arrived((up, down), up_in, down_in), v, inverse, held)
    for k, x in enumerate(PART_PLANES[0]):
        copies.append(pltpu.make_async_copy(held.at[:, k], out.at[:, x], sems.at[1 + k]))
        copies[-1].start()
    for copy in copies:
        copy.wait()


def back_scratch(part):
    return [pltpu.VMEM((8, 6 * 8 * len(PART_PLANES[part]), LANES), BF16)]


def front_scratch(count, with_field=True):
    shapes = [(2, 6 * count, LANES), (9, 3 * count, LANES), (6, 3 * count, LANES)]
    return [pltpu.VMEM(shape, BF16) for shape in shapes[: 3 if with_field else 2]]


def call(kernel, name, ins, outs, scratch, in_space=pltpu.VMEM, out_space=pltpu.VMEM):
    ins = [pltpu.with_memory_space_constraint(array, in_space) for array in ins]
    return pl.pallas_call(
        kernel,
        name=name,
        out_shape=[out_space(shape, dtype) for shape, dtype in outs],
        in_specs=[pl.BlockSpec(memory_space=in_space)] * len(ins),
        out_specs=[pl.BlockSpec(memory_space=out_space)] * len(outs),
        scratch_shapes=scratch,
        compiler_params=pltpu.CompilerParams(vmem_limit_bytes=24 * 1024 * 1024),
    )(*ins)


def wall_pairings(count):
    even = [(i, i + 1) for i in range(0, count - 1, 2)]
    odd = [(i, i + 1) for i in range(1, count - 1, 2)]
    return [pairs + [(b, a) for a, b in pairs] for pairs in (even, odd) if pairs]


def swap_edges(edge):
    return [lax.ppermute(edge, "col", way) for way in wall_pairings(lax.axis_size("col"))]


def local(adjoint_field, base_flow, metric_diag, metric_cross, jacobian):
    early_pack, late_pack = Packed(EARLY), Packed(LATE)
    bases, rho = wall_bases()
    block = adjoint_field.shape[1:]
    field = ((3,) + block, F32)
    kept_shapes = [
        ((9, 6 * QQ, LANES), BF16),
        ((6, 4 * XY, LANES), BF16),
        ((6, XY, LANES), F32),
    ]
    edge_shape = ((8, LANES), F32)
    spans = lax.axis_size("span")
    ahead = [(i, (i + 1) % spans) for i in range(spans)]
    back_way = [(b, a) for a, b in ahead]

    def sums(fields, part):
        return [((fields, len(PART_PLANES[part])) + block[1:], F32), edge_shape]

    def exchange(fields, outer, outer_edge, operands):
        outer_edges = swap_edges(outer_edge)
        inner, inner_edge = call(
            functools.partial(inner_kernel, len(operands) > 5, late_pack),
            "inner_planes",
            operands,
            sums(fields, 1),
            back_scratch(1),
        )
        up, down = call(
            functools.partial(planes_kernel, len(outer_edges)),
            "planes",
            [outer] + outer_edges + [inner_edge],
            [((fields,) + block[1:], F32)] * 2,
            [],
        )
        inner_edges = swap_edges(inner_edge)
        up_in, down_in = lax.ppermute(up, "span", ahead), lax.ppermute(down, "span", back_way)
        return [up, down, up_in, down_in], inner, inner_edges

    early, late = (jnp.asarray(pack.array, BF16) for pack in (early_pack, late_pack))
    ins = [jnp.asarray(bases), base_flow, adjoint_field, early]
    ins += [metric_diag, metric_cross, jacobian, late]
    v, early, late, z_forward, z_back, jac, w, u, metric, *kept, outer, outer_edge = call(
        functools.partial(first_kernel, early_pack, rho),
        "first_operator",
        ins,
        [field, (early.shape, BF16), (late.shape, BF16)]
        + [((6, 2 * LANES, LANES), BF16), ((2, 512, LANES), BF16)]
        + [(block, F32), ((XY, LANES), F32)]
        + [((9, QQ, LANES), F32), ((6, 2, XY, LANES), F32)]
        + kept_shapes
        + sums(4, 0),
        [
            pltpu.VMEM(bases.shape, F32),
            pltpu.VMEM((3,) + block, F32),
            pltpu.VMEM((3,) + block, BF16),
            pltpu.VMEM((3,) + block, BF16),
            pltpu.SemaphoreType.DMA((len(ins),)),
        ]
        + back_scratch(0)
        + front_scratch(XY)
        + front_scratch(XY, False),
        in_space=pltpu.HBM,
    )
    planes, inner, inner_edges = exchange(4, outer, outer_edge, kept + [z_back, late, jac, w])
    half = [pltpu.VMEM((3, 2, 8 * len(planes), LANES), F32) for planes in PART_PLANES]
    inner_inverse, *prepared = call(
        functools.partial(prepare_kernel, len(inner_edges)),
        "prepare",
        [v, z_forward, inner] + inner_edges,
        [
            ((6,) + block[1:], F32),
            ((9, 144, LANES), BF16),
            ((6, 144, LANES), BF16),
            ((6, 48, LANES), F32),
        ],
        [half[1], front_scratch(48)[0]],
    )
    inverse, *kept, outer, outer_edge = call(
        functools.partial(second_kernel, early_pack),
        "second_operator",
        [v, z_forward, z_back, early, u, metric] + prepared + planes,
        [((2,) + block[1:], F32)] + kept_shapes + sums(3, 0),
        back_scratch(0) + front_scratch(16) + [half[0]],
    )
    planes, inner, inner_edges = exchange(3, outer, outer_edge, kept + [z_back, late])
    (done,) = call(
        functools.partial(advance_inner_kernel, len(inner_edges)),
        "advance_inner",
        [v, inner_inverse, inner] + inner_edges,
        [((3, 6) + block[1:], F32)],
        [],
    )
    (out,) = call(
        advance_kernel,
        "advance",
        [v, inverse, done] + planes,
        [field],
        [pltpu.VMEM((3, 2) + block[1:], F32), pltpu.SemaphoreType.DMA((3,))],
        out_space=pltpu.HBM,
    )
    return out


def solution(mesh):
    in_specs = (
        P(None, "span", None, "col"),
        P(None, "span", None, "col"),
        P(None, "span", None, "col"),
        P(None, "span", None, "col"),
        P("span", None, "col"),
    )
    out_specs = P(None, "span", None, "col")
    return jax.shard_map(local, mesh=mesh, in_specs=in_specs, out_specs=out_specs, check_vma=False)
```
